32 devices in a mesh: space: 16 (over z, y, x), rep: 2 (over core).
Axes of the slice: x: 2, y: 2, z: 4, core: 2. Of those that a mesh axis runs over, the one named last changes fastest.
Arguments:
- features: bfloat16 [2, 64, 64, 512], P('rep', 'space'), may hold values from -6 to 6
- neighbours: int32 [2, 64, 26], P('rep', 'space'), may hold values from -1 to 35, as said below
- send_list: int32 [2, 16, 2, 16], P('rep', 'space'), may hold values from -1 to 3, as said below
- w_fine: bfloat16 [64, 1728], replicated, may hold values from -0.15625 to 0.15625
- w_down: bfloat16 [64, 512], replicated, may hold values from -0.25 to 0.25
- w_coarse: bfloat16 [64, 1728], replicated, may hold values from -0.15625 to 0.15625
- w_up: bfloat16 [64, 512], replicated, may hold values from -0.75 to 0.75
- cotangent: bfloat16 [2, 64, 64, 512], P('rep', 'space'), may hold values from -6 to 6
Outputs:
- decoded: bfloat16 [2, 64, 64, 512], P('rep', 'space')
- grad_fine: float32 [64, 1728], replicated
- grad_down: float32 [64, 512], replicated
- grad_coarse: float32 [64, 1728], replicated
- grad_up: float32 [64, 512], replicated
The draws below stay inside these ranges and needn't reach their ends.
Inputs may be any that keep to these rules, and one draw needn't show every extreme that they name: `neighbours`: A scene is a corridor 4 block positions across in the second and third dimensions; device d holds the occupied positions whose first coordinate lies in 4 d .. 4 d + 3, in Morton order. Entries follow true adjacency: below 4 a block of the same device, 4 + s (s < 4**2) the block of device d - 1 in slot s of its side 0, 4 + 4**2 + s the block of device d + 1 in slot s of its side 1, -1 an empty or outside position. In every slab the positions (0, 3, 3) and (3, 3, 3) are occupied and (3, 0, 0) is empty. send_list[d, 0, y * 4 + z] is device d's block at the last first-coordinate plane of its slab and position (y, z), send_list[d, 1, y * 4 + z] the one at the first plane; -1 where that position is empty.
All inputs are finite; a program needn't handle non-finite values.
Results may differ from the reference program's by a relative error of at most 0.007.
Values may be sent and summed in bfloat16 or wider, within the bound.
A program may use at most 128 MiB of HBM per device.

```python
import jax
import jax.numpy as jnp
from jax import lax

CH = 64
EDGE = 8
BLK_DEV = 4
BLOCKS = 64
SCENES = 2


DIRECTIONS = [(a, c, e) for a in (-1, 0, 1) for c in (-1, 0, 1) for e in (-1, 0, 1) if (a, c, e) != (0, 0, 0)]


def morton(xs, ys, zs):
    return (xs & 1) << 2 | (ys & 1) << 1 | zs & 1 | (xs >> 1 & 1) << 5 | (ys >> 1 & 1) << 4 | (zs >> 1 & 1) << 3


def corridor_layout(key):
    devices = BLOCKS // BLK_DEV
    cells = jnp.arange(64, dtype=jnp.int32)
    cell_x = cells >> 2 & 1 | (cells >> 5 & 1) << 1
    cell_y = cells >> 1 & 1 | (cells >> 4 & 1) << 1
    cell_z = cells & 1 | (cells >> 3 & 1) << 1
    step_x = jnp.array([d[0] for d in DIRECTIONS], dtype=jnp.int32)
    step_y = jnp.array([d[1] for d in DIRECTIONS], dtype=jnp.int32)
    step_z = jnp.array([d[2] for d in DIRECTIONS], dtype=jnp.int32)

    def one_slab(slab_key):
        ranks = jax.random.permutation(slab_key, 64).astype(jnp.int32)
        forced = (cells == 27) | (cells == 63)
        score = jnp.where(forced, -1, jnp.where(cells == 36, 64, ranks)).astype(jnp.int32)
        order = jnp.argsort(score, stable=True).astype(jnp.int32)
        return jnp.sort(order[:BLK_DEV]).astype(jnp.int32)

    def slab_grid(chosen):
        return jnp.full((64,), -1, jnp.int32).at[chosen].set(jnp.arange(BLK_DEV, dtype=jnp.int32))

    def one_scene(scene_key):
        chosen = jax.vmap(one_slab)(jax.random.split(scene_key, devices))
        grids = jax.vmap(slab_grid)(chosen)
        empty_row = jnp.full((1, 64), -1, jnp.int32)
        lower_grids = jnp.concatenate([empty_row, grids[:-1]], axis=0).reshape(-1)
        upper_grids = jnp.concatenate([grids[1:], empty_row], axis=0).reshape(-1)
        flat_grids = grids.reshape(-1)
        new_x = jnp.take(cell_x, chosen)[:, :, None] + step_x[None, None, :]
        new_y = jnp.take(cell_y, chosen)[:, :, None] + step_y[None, None, :]
        new_z = jnp.take(cell_z, chosen)[:, :, None] + step_z[None, None, :]
        inside = (new_y >= 0) & (new_y < 4) & (new_z >= 0) & (new_z < 4)
        clip_x = jnp.clip(new_x, 0, 3)
        clip_y = jnp.clip(new_y, 0, 3)
        clip_z = jnp.clip(new_z, 0, 3)
        base = (jnp.arange(devices, dtype=jnp.int32) * 64)[:, None, None]
        local_val = jnp.take(flat_grids, base + morton(clip_x, clip_y, clip_z))
        lower_val = jnp.take(lower_grids, base + morton(3, clip_y, clip_z))
        upper_val = jnp.take(upper_grids, base + morton(0, clip_y, clip_z))
        slot = clip_y * 4 + clip_z
        same = (new_x >= 0) & (new_x < 4)
        remote = jnp.where(new_x < 0, jnp.where(lower_val >= 0, BLK_DEV + slot, -1), jnp.where(upper_val >= 0, BLK_DEV + 16 + slot, -1))
        table = jnp.where(inside, jnp.where(same, local_val, remote), -1).astype(jnp.int32)
        positions = jnp.arange(16, dtype=jnp.int32)
        upper_ids = grids[:, morton(3, positions // 4, positions % 4)]
        lower_ids = grids[:, morton(0, positions // 4, positions % 4)]
        sends = jnp.stack([upper_ids, lower_ids], axis=1).astype(jnp.int32)
        return (table.reshape(BLOCKS, 26), sends)
    scene_keys = jax.random.split(jax.random.fold_in(key, 7), SCENES)
    return jax.vmap(one_scene)(scene_keys)


def draw_neighbours(key, part):
    return corridor_layout(key)[0]


def draw_send_list(key, part):
    return corridor_layout(key)[1]


def shard_levels(rng, shape, shards, smallest, largest):
    def one(position, blocks):
        draws = jax.random.uniform(jax.random.fold_in(jax.random.fold_in(rng, 6), position), (blocks,), jnp.float32, smallest / len(shards), largest / len(shards))
        return jnp.repeat(jnp.exp(draws), shape[position] // blocks).reshape((-1,) + (1,) * (len(shape) - position - 1))

    level = one(*shards[0])
    for cut in shards[1:]:
        level = level * one(*cut)
    return level


def noise(stream_key, extent, width, bound, cuts=(), held_as=jnp.bfloat16):
    loudness = shard_levels(stream_key, extent, cuts, -0.22, 0.18) if cuts else 1.0
    entries = jax.random.normal(stream_key, extent, jnp.float32) * width * loudness
    return jnp.minimum(jnp.maximum(entries, -bound), bound).astype(held_as)


def setup_inputs(seed: int = 0) -> dict:
    streams_of = jax.random.split(jax.random.key(seed), 9)
    features = noise(streams_of[0], (SCENES, BLOCKS, CH, EDGE**3), 1.0, 6.0, ((0, 2), (1, 16)))
    neighbours = draw_neighbours(jax.random.fold_in(streams_of[8], 71), 0)
    send_list = draw_send_list(jax.random.fold_in(streams_of[8], 71), 0)
    w_fine = noise(streams_of[3], (CH, 27 * CH), (27 * CH) ** -0.5, 0.15625)
    w_down = noise(streams_of[4], (CH, 8 * CH), (8 * CH) ** -0.5, 0.25)
    w_coarse = noise(streams_of[5], (CH, 27 * CH), (27 * CH) ** -0.5, 0.15625)
    w_up = noise(streams_of[6], (CH, 8 * CH), CH ** -0.5, 0.75)
    cotangent = noise(streams_of[7], (SCENES, BLOCKS, CH, EDGE**3), 1.0, 6.0, ((0, 2), (1, 16)))
    return {"features": features, "neighbours": neighbours, "send_list": send_list, "w_fine": w_fine, "w_down": w_down, "w_coarse": w_coarse, "w_up": w_up, "cotangent": cotangent}


DIRECTIONS = [(a, c, e) for a in (-1, 0, 1) for c in (-1, 0, 1) for e in (-1, 0, 1) if (a, c, e) != (0, 0, 0)]

def silu_slope(values):
    sig = jax.nn.sigmoid(values)
    return sig * (1.0 + values * (1.0 - sig))

def source_range(step, side):
    if step < 0:
        return slice(side - 1, side)
    if step == 0:
        return slice(0, side)
    return slice(0, 1)

def target_range(step, side):
    if step < 0:
        return slice(0, 1)
    if step == 0:
        return slice(1, side + 1)
    return slice(side + 1, side + 2)

def assemble(own_blocks, combined, sources, side):
    count, channels = (own_blocks.shape[0], own_blocks.shape[1])
    cubes = combined.reshape(combined.shape[0], channels, side, side, side)
    padded = jnp.zeros((count, channels, side + 2, side + 2, side + 2), own_blocks.dtype)
    padded = padded.at[:, :, 1:side + 1, 1:side + 1, 1:side + 1].set(own_blocks.reshape(count, channels, side, side, side))
    for k, (a, c, e) in enumerate(DIRECTIONS):
        part_cells = cubes[:, :, source_range(a, side), source_range(c, side), source_range(e, side)]
        source_ids = sources[:, k]
        gathered = jnp.take(part_cells, jnp.maximum(source_ids, 0), axis=0)
        gathered = jnp.where((source_ids >= 0)[:, None, None, None, None], gathered, jnp.zeros_like(gathered))
        padded = padded.at[:, :, target_range(a, side), target_range(c, side), target_range(e, side)].set(gathered)
    return padded

def lattice_columns(padded, side):
    count, channels = (padded.shape[0], padded.shape[1])
    parts_list = [padded[:, :, a:a + side, c:c + side, e:e + side].reshape(count, channels, side ** 3) for a in range(3) for c in range(3) for e in range(3)]
    return jnp.concatenate(parts_list, axis=1)

def spread_back(back_cols, side):
    count = back_cols.shape[0]
    channels = back_cols.shape[1] // 27
    result = jnp.zeros((count, channels, side + 2, side + 2, side + 2), back_cols.dtype)
    for a in range(3):
        for c in range(3):
            for e in range(3):
                offset = 9 * a + 3 * c + e
                piece = back_cols[:, offset * channels:(offset + 1) * channels].reshape(count, channels, side, side, side)
                result = result.at[:, :, a:a + side, c:c + side, e:e + side].add(piece)
    return result

def to_patches(field, side):
    count, channels = (field.shape[0], field.shape[1])
    half = side // 2
    shaped = field.reshape(count, channels, half, 2, half, 2, half, 2).transpose(0, 3, 5, 7, 1, 2, 4, 6)
    return shaped.reshape(count, 8 * channels, half ** 3)

def from_patches(values, half):
    count = values.shape[0]
    channels = values.shape[1] // 8
    shaped = values.reshape(count, 2, 2, 2, channels, half, half, half).transpose(0, 4, 5, 1, 6, 2, 7, 3)
    return shaped.reshape(count, channels, 8 * half ** 3)

def apply_conv(weight, halo, side):
    count = halo.shape[0]
    grouped = halo.reshape((count // 16, 16) + halo.shape[1:])

    def conv_step(pad_group):
        return jnp.einsum('ok,gkv->gov', weight.astype(jnp.float32), lattice_columns(pad_group, side).astype(jnp.float32))
    return lax.map(conv_step, grouped).reshape(count, weight.shape[0], side ** 3)

def conv_weights(delta, halo, side):
    count = halo.shape[0]
    channels = halo.shape[1]
    grouped = halo.reshape((count // 16, 16) + halo.shape[1:])
    delta_groups = delta.reshape((count // 16, 16) + delta.shape[1:])

    def weight_step(total, pair):
        pad_group, delta_group = pair
        cols = lattice_columns(pad_group, side).astype(jnp.float32)
        return (total + jnp.einsum('gov,gkv->ok', delta_group.astype(jnp.float32), cols), None)
    total, _ = lax.scan(weight_step, jnp.zeros((channels, 27 * channels), jnp.float32), (grouped, delta_groups))
    return total

def apply_adjoint(weight, delta, side):
    count = delta.shape[0]
    delta_groups = delta.reshape((count // 16, 16) + delta.shape[1:])

    def adjoint_step(delta_group):
        back_cols = jnp.einsum('ok,gov->gkv', weight.astype(jnp.float32), delta_group.astype(jnp.float32))
        return spread_back(back_cols, side)
    result = lax.map(adjoint_step, delta_groups)
    return result.reshape((count,) + result.shape[2:])

def halo_adjoint(back_pad, sources, side):
    count, channels = (back_pad.shape[0], back_pad.shape[1])
    totals = jnp.zeros((count + 1, channels, side, side, side), back_pad.dtype)
    for k, (a, c, e) in enumerate(DIRECTIONS):
        piece = back_pad[:, :, target_range(a, side), target_range(c, side), target_range(e, side)]
        source_ids = jnp.where(sources[:, k] >= 0, sources[:, k], count).astype(jnp.int32)
        totals = totals.at[source_ids, :, source_range(a, side), source_range(c, side), source_range(e, side)].add(piece)
    centre = back_pad[:, :, 1:side + 1, 1:side + 1, 1:side + 1]
    return (centre + totals[:count]).reshape(count, channels, side ** 3)

def global_sources(table, sends):
    devices = BLOCKS // BLK_DEV
    slots = sends.shape[2]
    owner = (jnp.arange(BLOCKS, dtype=jnp.int32) // BLK_DEV)[:, None]
    remote = jnp.clip(table - BLK_DEV, 0, 2 * slots - 1).astype(jnp.int32)
    side_id = remote // slots
    slot_id = remote % slots
    peer = jnp.clip(owner - 1 + 2 * side_id, 0, devices - 1).astype(jnp.int32)
    remote_id = peer * BLK_DEV + sends[peer, side_id, slot_id]
    local_id = owner * BLK_DEV + table
    return jnp.where(table < 0, -1, jnp.where(table < BLK_DEV, local_id, remote_id)).astype(jnp.int32)

def reference(features, neighbours, send_list, w_fine, w_down, w_coarse, w_up, cotangent):
    f32 = jnp.float32
    coarse_side = EDGE // 2
    channels = w_fine.shape[0]
    grad_fine = jnp.zeros((channels, 27 * channels), f32)
    grad_down = jnp.zeros((channels, 8 * channels), f32)
    grad_coarse = jnp.zeros((channels, 27 * channels), f32)
    grad_up = jnp.zeros((channels, 8 * channels), f32)
    decoded_list = []
    for scene in range(SCENES):
        sources = global_sources(neighbours[scene], send_list[scene])
        fine_in = features[scene]
        halo0 = assemble(fine_in, fine_in, sources, EDGE)
        fine_pre = apply_conv(w_fine, halo0, EDGE)
        hidden0 = jax.nn.silu(fine_pre).astype(jnp.bfloat16)
        patches0 = to_patches(hidden0, EDGE)
        coarse_pre = jnp.einsum('ok,bkv->bov', w_down.astype(f32), patches0.astype(f32))
        hidden1 = jax.nn.silu(coarse_pre).astype(jnp.bfloat16)
        halo1 = assemble(hidden1, hidden1, sources, coarse_side)
        coarse_conv = apply_conv(w_coarse, halo1, coarse_side)
        gated = jax.nn.silu(coarse_conv).astype(jnp.bfloat16)
        up_terms = from_patches(jnp.einsum('ik,biv->bkv', w_up.astype(f32), gated.astype(f32)), coarse_side)
        decoded_list.append((hidden0.astype(f32) + up_terms).astype(jnp.bfloat16))
        cot_patch = to_patches(cotangent[scene], EDGE).astype(f32)
        grad_up = grad_up + jnp.einsum('biv,bkv->ik', gated.astype(f32), cot_patch)
        up_back = jnp.einsum('ik,bkv->biv', w_up.astype(f32), cot_patch)
        delta_up = (up_back * silu_slope(coarse_conv)).astype(jnp.bfloat16)
        grad_coarse = grad_coarse + conv_weights(delta_up, halo1, coarse_side)
        back_pad = apply_adjoint(w_coarse, delta_up, coarse_side)
        grad_hidden1 = halo_adjoint(back_pad, sources, coarse_side)
        delta_down = (grad_hidden1 * silu_slope(coarse_pre)).astype(jnp.bfloat16)
        grad_down = grad_down + jnp.einsum('bov,bkv->ok', delta_down.astype(f32), patches0.astype(f32))
        down_back = jnp.einsum('ok,bov->bkv', w_down.astype(f32), delta_down.astype(f32))
        grad_hidden0 = cotangent[scene].astype(f32) + from_patches(down_back, coarse_side)
        delta_fine = (grad_hidden0 * silu_slope(fine_pre)).astype(jnp.bfloat16)
        grad_fine = grad_fine + conv_weights(delta_fine, halo0, EDGE)
    factor = 1.0 / jnp.sqrt(jnp.asarray(SCENES * BLOCKS * EDGE ** 3, f32))
    return (jnp.stack(decoded_list), grad_fine * factor, grad_down * factor, grad_coarse * factor, grad_up * factor)
```

```python
import functools
import math

import jax
import jax.numpy as jnp
import numpy as np
from jax import lax
from jax.experimental import pallas as pl
from jax.experimental.pallas import tpu as pltpu
from jax.sharding import PartitionSpec as P

EDGE = 8
HALF = EDGE // 2
TILE = 128
F32 = jnp.float32
BF16 = jnp.bfloat16
MESH = pl.DeviceIdType.MESH


def spots(step, side):
    if step < 0:
        return [(side - 1, 0)]
    if step == 0:
        return [(v, v + 1) for v in range(side)]
    return [(0, side + 1)]


def fine_spread():
    table = np.zeros((9, 2, EDGE, EDGE, 2, TILE), np.float32)
    for j in (-1, 0, 1):
        for l in (-1, 0, 1):
            for y, py in spots(j, EDGE):
                for z, pz in spots(l, EDGE):
                    for x in range(2):
                        table[3 * (j + 1) + l + 1, x, y, z, x, (EDGE + 2) * py + pz] = 1
    return table.reshape(9 * 2 * EDGE * EDGE, 2 * TILE)


def coarse_spread():
    table = np.zeros((10, HALF, HALF, HALF, HALF, TILE), np.float32)
    for j in (-1, 0, 1):
        for l in (-1, 0, 1):
            for y, py in spots(j, HALF):
                for z, pz in spots(l, HALF):
                    for x in range(HALF):
                        table[3 * (j + 1) + l + 1, x, y, z, x, (HALF + 2) * py + pz] = 1
    return table.reshape(10 * HALF**3, HALF * TILE)


def pair_spread():
    centre = coarse_spread().reshape(10, HALF**3, HALF, TILE)[4]
    return np.concatenate([centre, np.roll(centre, 64, axis=-1)]).reshape(2 * HALF**3, HALF * TILE)


def patch_order():
    table = np.zeros((EDGE**3, EDGE**3), np.float32)
    for x in range(EDGE):
        for y in range(EDGE):
            for z in range(EDGE):
                part = 4 * (x % 2) + 2 * (y % 2) + z % 2
                cell = (x // 2 * HALF + y // 2) * HALF + z // 2
                table[(x * EDGE + y) * EDGE + z, part * HALF**3 + cell] = 1
    return table


def dot(a, b):
    return jnp.dot(a, b, preferred_element_type=F32)


def dot_t(a, b):
    return lax.dot_general(a, b, (((1,), (1,)), ((), ())), preferred_element_type=F32)


def split_dot(f, a, b):
    high = a.astype(BF16)
    low = (a - high.astype(F32)).astype(BF16)
    return f(high, b) + f(low, b)


def tiles(x):
    return [x[:, TILE * t : TILE * (t + 1)] for t in range(x.shape[1] // TILE)]


def turn(x, shift):
    shift = shift % TILE
    if shift == 0:
        return x
    return jnp.concatenate([pltpu.roll(t, shift, axis=1) for t in tiles(x)], axis=1)


def sigmoid(v):
    return 1.0 / (1.0 + jnp.exp(-v))


def placed(x, tile_count):
    rows = []
    for a in range(3):
        parts = []
        if a:
            parts.append(jnp.zeros((x.shape[0], a * TILE), x.dtype))
        parts.append(x)
        if a < 2:
            parts.append(jnp.zeros((x.shape[0], (2 - a) * TILE), x.dtype))
        rows.append(jnp.concatenate(parts, axis=1))
    return jnp.concatenate(rows, axis=0)


def body(
    peers,
    f_ref, nb_ref, sl_ref, cot_ref, wf_ref, wd_ref, wc_ref, wct_ref, wu_ref, wdt_ref, wut_ref,
    e0_ref, q0_ref, q2_ref, pm_ref,
    out_ref, grads_ref,
    x0, fh, fl, sl_lo, sl_hi, sm_lo, sm_hi, idx, r0, slope0, p2, c2, h1, h1_lo, h1_hi,
    cand, r1, rim, rim_lo, rim_hi, dg0, dgm, dgp, gh1, gh0,
    send_sem, recv_sem, local_sem,
):
    nb, ch = f_ref.shape[0], f_ref.shape[1]
    cells = HALF**3
    me = lax.axis_index("space")
    rep = lax.axis_index("rep")
    up = lax.rem(me + 1, peers)
    down = lax.rem(me + peers - 1, peers)

    barrier = pltpu.get_barrier_semaphore()
    for other in (up, down):
        pl.semaphore_signal(barrier, inc=1, device_id=(other, rep), device_id_type=MESH)
    pl.semaphore_wait(barrier, 2)

    def remote(src, dst, n, other):
        copy = pltpu.make_async_remote_copy(
            src_ref=src, dst_ref=dst, send_sem=send_sem.at[n], recv_sem=recv_sem.at[n],
            device_id=(other, rep), device_id_type=MESH,
        )
        copy.start()
        return copy

    last = f_ref.shape[2] - TILE
    first = [
        remote(sl_ref, sl_lo, 0, up),
        remote(sl_ref, sl_hi, 1, down),
        remote(f_ref.at[:, :, last:], fh.at[nb : 2 * nb], 2, up),
        remote(f_ref.at[:, :, :TILE], fl.at[nb : 2 * nb], 3, down),
    ]

    x0[:nb] = f_ref[...]
    x0[nb] = jnp.zeros(x0.shape[1:], BF16)
    fh[:nb] = f_ref[:, :, last:]
    fl[:nb] = f_ref[:, :, :TILE]
    fh[2 * nb] = jnp.zeros(fh.shape[1:], BF16)
    fl[2 * nb] = jnp.zeros(fl.shape[1:], BF16)

    def to_patches(src, dst, b):
        moved = dot(src, pm_ref[...]).astype(BF16)
        for part in range(8):
            dst[part * ch : (part + 1) * ch, b * cells : (b + 1) * cells] = moved[
                :, part * cells : (part + 1) * cells
            ]

    for b in range(nb):
        to_patches(cot_ref[b], c2, b)

    first[0].wait()
    first[1].wait()
    to_smem = [
        pltpu.make_async_copy(sl_lo, sm_lo, local_sem.at[0]),
        pltpu.make_async_copy(sl_hi, sm_hi, local_sem.at[1]),
    ]
    for copy in to_smem:
        copy.start()
    for copy in to_smem:
        copy.wait()
    slots = sl_ref.shape[1]
    none = 2 * nb
    for b in range(nb):
        for k in range(27):
            if k == 13:
                idx[b, k] = jnp.int32(b)
                continue
            v = nb_ref[b, k if k < 13 else k - 1]
            if k < 9:
                far = nb + sm_lo[0, jnp.clip(v - nb, 0, slots - 1)]
                v = jnp.where(v < 0, none, jnp.where(v < nb, v, far))
            elif k >= 18:
                far = nb + sm_hi[1, jnp.clip(v - nb - slots, 0, slots - 1)]
                v = jnp.where(v < 0, none, jnp.where(v < nb, v, far))
            else:
                v = jnp.where(v < 0, nb, v)
            idx[b, k] = v
    first[2].wait()
    first[3].wait()

    e0 = e0_ref[...]
    e0c = e0_ref[4 * TILE : 5 * TILE, :]
    for b in range(nb):
        rows = []
        for t in range(4):
            rows.append(
                jnp.concatenate(
                    [x0[idx[b, 9 + n], :, t * TILE : (t + 1) * TILE] for n in range(9)], axis=1
                )
            )
        inner = dot(jnp.concatenate(rows, axis=0), e0)
        low = dot(jnp.concatenate([fh[idx[b, n]] for n in range(9)], axis=1), e0[:, TILE:])
        high = dot(jnp.concatenate([fl[idx[b, 18 + n]] for n in range(9)], axis=1), e0[:, :TILE])
        pad = jnp.concatenate(
            [low] + [inner[t * ch : (t + 1) * ch] for t in range(4)] + [high], axis=1
        )
        for n in range(9):
            off = (EDGE + 2) * (n // 3 - 1) + n % 3 - 1
            r0[b, n * ch : (n + 1) * ch, :] = turn(pad, -off).astype(BF16)
        y = dot(wf_ref[...], r0[b])
        wide = EDGE * TILE
        v = sum(y[a * ch : (a + 1) * ch, a * TILE : a * TILE + wide] for a in range(3))
        s = sigmoid(v)
        slope0[b] = s * (1.0 + v * (1.0 - s))
        h = (v * s).astype(BF16)
        flat = jnp.concatenate(
            [dot_t(h[:, 2 * TILE * t : 2 * TILE * (t + 1)], e0c).astype(BF16) for t in range(4)],
            axis=1,
        )
        to_patches(flat, p2, b)

    coarse_pre = dot(wd_ref[...], p2[...])
    s = sigmoid(coarse_pre)
    slope_down = s * (1.0 + coarse_pre * (1.0 - s))
    hidden1 = (coarse_pre * s).astype(BF16)
    h1[...] = hidden1
    second = [remote(h1, h1_lo, 4, up), remote(h1, h1_hi, 5, down)]

    lane = lax.broadcasted_iota(jnp.int32, (ch, TILE), 1)
    left = lane < cells
    nothing = jnp.zeros((ch, TILE), F32)

    def candidates(value, table, base):
        for b in range(nb):
            x = value[:, (b // 2) * TILE : (b // 2 + 1) * TILE].astype(F32)
            swapped = pltpu.roll(x, cells, axis=1)
            on_left, on_right = (x, swapped) if b % 2 == 0 else (swapped, x)
            cand[table, 0, base + b] = jnp.where(left, on_left, nothing).astype(BF16)
            cand[table, 1, base + b] = jnp.where(left, nothing, on_right).astype(BF16)

    for table in range(3):
        candidates(hidden1, table, 0)
        for half in range(2):
            cand[table, half, none] = nothing.astype(BF16)
            if table == 1:
                for n in range(nb, 2 * nb):
                    cand[table, half, n] = nothing.astype(BF16)
    up_back = dot(wu_ref[...], c2[...])
    for copy in second:
        copy.wait()
    candidates(h1_lo[...], 0, nb)
    candidates(h1_hi[...], 2, nb)

    q0 = q0_ref[...]
    top = (HALF - 1) * TILE

    def sources(b, i):
        parts = []
        for t in range(5):
            x = cand[i, 0, idx[b, 9 * i + 2 * t]]
            if t < 4:
                x = x + cand[i, 1, idx[b, 9 * i + 2 * t + 1]]
            parts.append(x)
        return jnp.concatenate(parts, axis=1)

    pairs = nb // 2
    wide1 = HALF * TILE
    gated = []
    delta_up = []
    for p in range(pairs):
        pads = []
        for b in (2 * p, 2 * p + 1):
            pads.append(
                jnp.concatenate(
                    [
                        dot(sources(b, 0), q0[:, top:]),
                        dot(sources(b, 1), q0),
                        dot(sources(b, 2), q0[:, :TILE]),
                    ],
                    axis=1,
                )
            )
        pad = pads[0] + turn(pads[1], cells)
        for n in range(9):
            off = (HALF + 2) * (n // 3 - 1) + n % 3 - 1
            r1[p, n * ch : (n + 1) * ch, :] = turn(pad, -off).astype(BF16)
        y = dot(wc_ref[...], r1[p])
        v = sum(y[a * ch : (a + 1) * ch, a * TILE : a * TILE + wide1] for a in range(3))
        s = sigmoid(v)
        slope = s * (1.0 + v * (1.0 - s))
        gated.append(dot_t((v * s).astype(BF16), q2_ref[...]).astype(BF16))
        ub = split_dot(dot, up_back[:, p * TILE : (p + 1) * TILE], q2_ref[...])
        delta = (ub * slope).astype(BF16)
        delta_up.append(delta)
        turned = []
        for n in range(9):
            off = (HALF + 2) * (n // 3 - 1) + n % 3 - 1
            turned.append(turn(delta.astype(F32), off).astype(BF16))
        y = dot(wct_ref[...], jnp.concatenate(turned, axis=0))
        gap = jnp.zeros((ch, TILE), F32)
        back = (
            jnp.concatenate([y[:ch], gap, gap], axis=1)
            + jnp.concatenate([gap, y[ch : 2 * ch], gap], axis=1)
            + jnp.concatenate([gap, gap, y[2 * ch :]], axis=1)
        )
        rim[0, p] = back[:, :TILE].astype(BF16)
        rim[1, p] = back[:, -TILE:].astype(BF16)
        for h in range(2):
            b = 2 * p + h
            x = turn(back, -h * cells)
            dg0[b] = split_dot(dot_t, x[:, TILE : TILE + wide1], q0)
            dgm[b] = split_dot(dot_t, x[:, :TILE], q0[:, top:])
            dgp[b] = split_dot(dot_t, x[:, -TILE:], q0[:, :TILE])
    third = [remote(rim.at[0], rim_hi, 6, down), remote(rim.at[1], rim_lo, 7, up)]

    gated = jnp.concatenate(gated, axis=1)
    dec = (p2[...].astype(F32) + dot(wut_ref[...], gated)).astype(BF16)

    def from_patches(value, b):
        return jnp.concatenate(
            [value[n * ch : (n + 1) * ch, b * cells : (b + 1) * cells] for n in range(8)], axis=1
        )

    for b in range(nb):
        out_ref[b] = dot_t(from_patches(dec, b), pm_ref[...]).astype(BF16)
    taps = 9 * ch
    grad_coarse = sum(dot_t(placed(delta_up[p], HALF), r1[p]) for p in range(pairs))
    for a in range(3):
        grads_ref[:, (3 + a) * taps : (4 + a) * taps] = grad_coarse[a * ch : (a + 1) * ch]
    grads_ref[:, 6 * taps + 8 * ch : 6 * taps + 16 * ch] = dot_t(gated, c2[...])

    dg0[nb] = jnp.zeros(dg0.shape[1:], F32)
    dgm[none] = jnp.zeros(dg0.shape[1:], F32)
    dgp[none] = jnp.zeros(dg0.shape[1:], F32)
    for copy in third:
        copy.wait()
    for p in range(pairs):
        for h in range(2):
            x = turn(rim_hi[p].astype(F32), -h * cells).astype(BF16)
            dgm[nb + 2 * p + h] = dot_t(x, q0[:, top:])
            x = turn(rim_lo[p].astype(F32), -h * cells).astype(BF16)
            dgp[nb + 2 * p + h] = dot_t(x, q0[:, :TILE])
    for b in range(nb):
        sums = [nothing, nothing]
        for k in range(27):
            chunk = 8 - k % 9
            table = (dgp, dg0, dgm)[k // 9]
            t = chunk // 2
            sums[chunk % 2] = sums[chunk % 2] + table[idx[b, k], :, t * TILE : (t + 1) * TILE]
        gh1[:, b * cells : (b + 1) * cells] = sums[0][:, :cells] + sums[1][:, cells:]
    delta_down = (gh1[...] * slope_down).astype(BF16)
    grads_ref[:, 6 * taps : 6 * taps + 8 * ch] = dot_t(delta_down, p2[...])
    gh0[...] = c2[...].astype(F32) + dot(wdt_ref[...], delta_down)
    grad_fine = jnp.zeros((3 * ch, taps), F32)
    for b in range(nb):
        flat = dot_t(from_patches(gh0[...], b).astype(BF16), pm_ref[...]).astype(BF16)
        wide_grad = jnp.concatenate([dot(t, e0c) for t in tiles(flat)], axis=1)
        delta = (wide_grad * slope0[b]).astype(BF16)
        grad_fine = grad_fine + dot_t(placed(delta, EDGE), r0[b])
    for a in range(3):
        grads_ref[:, a * taps : (a + 1) * taps] = grad_fine[a * ch : (a + 1) * ch]


def shards(features, neighbours, send_list, w_fine, w_down, w_coarse, w_up, cotangent):
    nb, ch = features.shape[1], features.shape[2]
    cols = nb * HALF**3
    peers = lax.axis_size("space")
    taps = 9 * ch

    def stacked(w):
        return w.reshape(ch, 3, taps).transpose(1, 0, 2).reshape(3 * ch, taps)

    wct = w_coarse.reshape(ch, 3, 9, ch).transpose(1, 3, 2, 0).reshape(3 * ch, taps)
    consts = [jnp.asarray(t(), BF16) for t in (fine_spread, coarse_spread, pair_spread, patch_order)]
    vmem = pl.BlockSpec(memory_space=pltpu.VMEM)
    smem = pl.BlockSpec(memory_space=pltpu.SMEM)
    v = pltpu.VMEM
    width = 10 * HALF**3
    decoded, grads = pl.pallas_call(
        functools.partial(body, peers),
        out_shape=(
            jax.ShapeDtypeStruct(features.shape[1:], BF16),
            jax.ShapeDtypeStruct((ch, 6 * taps + 16 * ch), F32),
        ),
        in_specs=[vmem, smem] + [vmem] * 13,
        out_specs=(vmem, vmem),
        scratch_shapes=[
            v((nb + 1, ch, EDGE**3), BF16),
            v((2 * nb + 1, ch, TILE), BF16),
            v((2 * nb + 1, ch, TILE), BF16),
            v(send_list.shape[2:], jnp.int32),
            v(send_list.shape[2:], jnp.int32),
            pltpu.SMEM(send_list.shape[2:], jnp.int32),
            pltpu.SMEM(send_list.shape[2:], jnp.int32),
            pltpu.SMEM((nb, 27), jnp.int32),
            v((nb, taps, (EDGE + 2) * TILE), BF16),
            v((nb, ch, EDGE * TILE), F32),
            v((8 * ch, cols), BF16),
            v((8 * ch, cols), BF16),
            v((ch, cols), BF16),
            v((ch, cols), BF16),
            v((ch, cols), BF16),
            v((3, 2, 2 * nb + 1, ch, TILE), BF16),
            v((nb // 2, taps, (HALF + 2) * TILE), BF16),
            v((2, nb // 2, ch, TILE), BF16),
            v((nb // 2, ch, TILE), BF16),
            v((nb // 2, ch, TILE), BF16),
            v((nb + 1, ch, width), F32),
            v((2 * nb + 1, ch, width), F32),
            v((2 * nb + 1, ch, width), F32),
            v((ch, cols), F32),
            v((8 * ch, cols), F32),
            pltpu.SemaphoreType.DMA((8,)),
            pltpu.SemaphoreType.DMA((8,)),
            pltpu.SemaphoreType.DMA((2,)),
        ],
        compiler_params=pltpu.CompilerParams(
            collective_id=0, has_side_effects=True, vmem_limit_bytes=56 * 1024 * 1024
        ),
    )(
        features[0], neighbours[0], send_list[0, 0], cotangent[0],
        stacked(w_fine), w_down, stacked(w_coarse), wct, w_up, w_down.T, w_up.T, *consts,
    )
    factor = 1.0 / math.sqrt(lax.axis_size("rep") * peers * nb * EDGE**3)
    grads = lax.psum(grads, ("space", "rep")) * factor
    a, b, c = 3 * taps, 6 * taps, 6 * taps + 8 * ch
    return decoded[None], grads[:, :a], grads[:, b:c], grads[:, a:b], grads[:, c:]


def solution(mesh):
    in_specs = (
        P("rep", "space", None, None),
        P("rep", "space", None),
        P("rep", "space", None, None),
        P(),
        P(),
        P(),
        P(),
        P("rep", "space", None, None),
    )
    out_specs = (P("rep", "space", None, None), P(), P(), P(), P())
    return jax.shard_map(shards, mesh=mesh, in_specs=in_specs, out_specs=out_specs, check_vma=False)
```

```python
import functools
import math

import jax
import jax.numpy as jnp
import numpy as np
from jax import lax
from jax.experimental import pallas as pl
from jax.experimental.pallas import tpu as pltpu
from jax.sharding import PartitionSpec as P

EDGE = 8
HALF = EDGE // 2
TILE = 128
F32 = jnp.float32
BF16 = jnp.bfloat16
MESH = pl.DeviceIdType.MESH


def spots(step, side):
    if step < 0:
        return [(side - 1, 0)]
    if step == 0:
        return [(v, v + 1) for v in range(side)]
    return [(0, side + 1)]


def fine_spread():
    table = np.zeros((9, 2, EDGE, EDGE, 2, TILE), np.float32)
    for j in (-1, 0, 1):
        for l in (-1, 0, 1):
            for y, py in spots(j, EDGE):
                for z, pz in spots(l, EDGE):
                    for x in range(2):
                        table[3 * (j + 1) + l + 1, x, y, z, x, (EDGE + 2) * py + pz] = 1
    return table.reshape(9 * 2 * EDGE * EDGE, 2 * TILE)


def coarse_spread():
    table = np.zeros((10, HALF, HALF, HALF, HALF, TILE), np.float32)
    for j in (-1, 0, 1):
        for l in (-1, 0, 1):
            for y, py in spots(j, HALF):
                for z, pz in spots(l, HALF):
                    for x in range(HALF):
                        table[3 * (j + 1) + l + 1, x, y, z, x, (HALF + 2) * py + pz] = 1
    return table.reshape(10 * HALF**3, HALF * TILE)


def pair_spread():
    centre = coarse_spread().reshape(10, HALF**3, HALF, TILE)[4]
    return np.concatenate([centre, np.roll(centre, 64, axis=-1)]).reshape(2 * HALF**3, HALF * TILE)


def patch_order():
    table = np.zeros((EDGE**3, EDGE**3), np.float32)
    for x in range(EDGE):
        for y in range(EDGE):
            for z in range(EDGE):
                part = 4 * (x % 2) + 2 * (y % 2) + z % 2
                cell = (x // 2 * HALF + y // 2) * HALF + z // 2
                table[(x * EDGE + y) * EDGE + z, part * HALF**3 + cell] = 1
    return table


def dot(a, b):
    return jnp.dot(a, b, preferred_element_type=F32)


def dot_t(a, b):
    return lax.dot_general(a, b, (((1,), (1,)), ((), ())), preferred_element_type=F32)


def split_dot(f, a, b):
    high = a.astype(BF16)
    low = (a - high.astype(F32)).astype(BF16)
    return f(high, b) + f(low, b)


def tiles(x):
    return [x[:, TILE * t : TILE * (t + 1)] for t in range(x.shape[1] // TILE)]


def turn(x, shift):
    shift = shift % TILE
    if shift == 0:
        return x
    return jnp.concatenate([pltpu.roll(t, shift, axis=1) for t in tiles(x)], axis=1)


def sigmoid(v):
    return 1.0 / (1.0 + jnp.exp(-v))


def placed(x, tile_count):
    rows = []
    for a in range(3):
        parts = []
        if a:
            parts.append(jnp.zeros((x.shape[0], a * TILE), x.dtype))
        parts.append(x)
        if a < 2:
            parts.append(jnp.zeros((x.shape[0], (2 - a) * TILE), x.dtype))
        rows.append(jnp.concatenate(parts, axis=1))
    return jnp.concatenate(rows, axis=0)


def group_width(count, peers):
    groups = peers // 2
    return -(-count // (groups * TILE)) * TILE


class Sum:
    def __init__(self, peers, factor, grads, part, pair, mid, got, full, send, recv):
        self.peers, self.factor = peers, factor
        self.grads, self.part, self.pair, self.mid, self.got, self.full = grads, part, pair, mid, got, full
        self.send, self.recv = send, recv
        self.me, self.rep = lax.axis_index("space"), lax.axis_index("rep")
        self.groups = peers // 2
        self.width = part.shape[2]

    def copy(self, src, dst, n, chip, core):
        return pltpu.make_async_remote_copy(
            src_ref=src, dst_ref=dst, send_sem=self.send.at[n], recv_sem=self.recv.at[n],
            device_id=(chip, core), device_id_type=MESH,
        )

    def pair_copy(self):
        other = 1 - self.rep
        src = self.part.at[pl.ds(other * self.peers, self.peers)]
        return self.copy(src, self.pair, 0, self.me, other)

    def share_copy(self, o):
        chip = lax.rem(self.me + o, self.peers)
        return self.copy(self.mid.at[chip], self.got.at[o], o, chip, self.rep)

    def total_copy(self, o, owner):
        chip = lax.rem(self.me + o, self.peers)
        spot = self.full.at[self.rep * self.peers + owner]
        return self.copy(spot, spot, self.peers + o, chip, self.rep)

    def core_copy(self, o):
        owner = lax.rem(self.me + self.peers - o, self.peers)
        spot = self.full.at[self.rep * self.peers + owner]
        return self.copy(spot, spot, 2 * self.peers + o, self.me, 1 - self.rep)

    def each(self, start, act):
        lax.fori_loop(start, self.peers, lambda o, c: (act(o), c)[1], 0)

    def begin(self):
        w = self.width
        for row in range(4):
            for col in range(self.groups):
                self.part[row * self.groups + col] = self.grads[
                    16 * row : 16 * row + 16, col * w : (col + 1) * w
                ].astype(BF16)
        self.pair_copy().start()

    def scatter(self):
        self.pair_copy().wait()
        mine = self.part[pl.ds(self.rep * self.peers, self.peers)]
        self.mid[...] = (mine.astype(F32) + self.pair[...].astype(F32)).astype(BF16)
        self.each(1, lambda o: self.share_copy(o).start())

    def gather(self):
        self.each(1, lambda o: self.share_copy(o).wait())
        total = self.mid[self.me].astype(F32)
        for o in range(1, self.peers):
            total = total + self.got[o].astype(F32)
        self.full[self.rep * self.peers + self.me] = (total * self.factor).astype(BF16)
        self.core_copy(0).start()
        self.each(1, lambda o: self.total_copy(o, self.me).start())

    def finish(self, out):
        def pass_on(o):
            owner = lax.rem(self.me + self.peers - o, self.peers)
            self.total_copy(o, owner).wait_recv()
            self.core_copy(o).start()

        self.each(1, pass_on)
        self.each(1, lambda o: self.total_copy(o, self.me).wait_send())
        self.each(0, lambda o: self.core_copy(o).wait())
        w = self.width
        for row in range(4):
            for col in range(self.groups):
                end = min((col + 1) * w, out.shape[1])
                if end > col * w:
                    out[16 * row : 16 * row + 16, col * w : end] = self.full[
                        row * self.groups + col, :, : end - col * w
                    ].astype(F32)


def body(
    peers, factor,
    f_ref, nb_ref, sl_ref, cot_ref, wf_ref, wd_ref, wc_ref, wct_ref, wu_ref, wdt_ref, wut_ref,
    e0_ref, q0_ref, q2_ref, pm_ref,
    out_ref, second_ref, first_ref,
    x0, fh, fl, sl_lo, sl_hi, sm_lo, sm_hi, idx, r0, slope0, p2, c2, h1, h1_lo, h1_hi,
    cand, r1, rim, rim_lo, rim_hi, dg0, dgm, dgp, gh1, gh0,
    send_sem, recv_sem, local_sem,
    *sums,
):
    second_sum = Sum(peers, factor, *sums[:8])
    first_sum = Sum(peers, factor, *sums[8:])
    second_grads, first_grads = second_sum.grads, first_sum.grads
    nb, ch = f_ref.shape[0], f_ref.shape[1]
    cells = HALF**3
    me = lax.axis_index("space")
    rep = lax.axis_index("rep")
    up = lax.rem(me + 1, peers)
    down = lax.rem(me + peers - 1, peers)

    barrier = pltpu.get_barrier_semaphore()

    def greet(o, carry):
        other = lax.rem(me + o, peers)
        pl.semaphore_signal(barrier, inc=1, device_id=(other, rep), device_id_type=MESH)
        return carry

    lax.fori_loop(1, peers, greet, 0)
    pl.semaphore_signal(barrier, inc=1, device_id=(me, 1 - rep), device_id_type=MESH)
    pl.semaphore_wait(barrier, peers)

    def remote(src, dst, n, other):
        copy = pltpu.make_async_remote_copy(
            src_ref=src, dst_ref=dst, send_sem=send_sem.at[n], recv_sem=recv_sem.at[n],
            device_id=(other, rep), device_id_type=MESH,
        )
        copy.start()
        return copy

    last = f_ref.shape[2] - TILE
    first = [
        remote(sl_ref, sl_lo, 0, up),
        remote(sl_ref, sl_hi, 1, down),
        remote(f_ref.at[:, :, last:], fh.at[nb : 2 * nb], 2, up),
        remote(f_ref.at[:, :, :TILE], fl.at[nb : 2 * nb], 3, down),
    ]

    x0[:nb] = f_ref[...]
    x0[nb] = jnp.zeros(x0.shape[1:], BF16)
    fh[:nb] = f_ref[:, :, last:]
    fl[:nb] = f_ref[:, :, :TILE]
    fh[2 * nb] = jnp.zeros(fh.shape[1:], BF16)
    fl[2 * nb] = jnp.zeros(fl.shape[1:], BF16)

    def to_patches(src, dst, b):
        moved = dot(src, pm_ref[...]).astype(BF16)
        for part in range(8):
            dst[part * ch : (part + 1) * ch, b * cells : (b + 1) * cells] = moved[
                :, part * cells : (part + 1) * cells
            ]

    for b in range(nb):
        to_patches(cot_ref[b], c2, b)

    first[0].wait()
    first[1].wait()
    to_smem = [
        pltpu.make_async_copy(sl_lo, sm_lo, local_sem.at[0]),
        pltpu.make_async_copy(sl_hi, sm_hi, local_sem.at[1]),
    ]
    for copy in to_smem:
        copy.start()
    for copy in to_smem:
        copy.wait()
    slots = sl_ref.shape[1]
    none = 2 * nb
    for b in range(nb):
        for k in range(27):
            if k == 13:
                idx[b, k] = jnp.int32(b)
                continue
            v = nb_ref[b, k if k < 13 else k - 1]
            if k < 9:
                far = nb + sm_lo[0, jnp.clip(v - nb, 0, slots - 1)]
                v = jnp.where(v < 0, none, jnp.where(v < nb, v, far))
            elif k >= 18:
                far = nb + sm_hi[1, jnp.clip(v - nb - slots, 0, slots - 1)]
                v = jnp.where(v < 0, none, jnp.where(v < nb, v, far))
            else:
                v = jnp.where(v < 0, nb, v)
            idx[b, k] = v
    first[2].wait()
    first[3].wait()

    e0 = e0_ref[...]
    e0c = e0_ref[4 * TILE : 5 * TILE, :]
    for b in range(nb):
        rows = []
        for t in range(4):
            rows.append(
                jnp.concatenate(
                    [x0[idx[b, 9 + n], :, t * TILE : (t + 1) * TILE] for n in range(9)], axis=1
                )
            )
        inner = dot(jnp.concatenate(rows, axis=0), e0)
        low = dot(jnp.concatenate([fh[idx[b, n]] for n in range(9)], axis=1), e0[:, TILE:])
        high = dot(jnp.concatenate([fl[idx[b, 18 + n]] for n in range(9)], axis=1), e0[:, :TILE])
        pad = jnp.concatenate(
            [low] + [inner[t * ch : (t + 1) * ch] for t in range(4)] + [high], axis=1
        )
        for n in range(9):
            off = (EDGE + 2) * (n // 3 - 1) + n % 3 - 1
            r0[b, n * ch : (n + 1) * ch, :] = turn(pad, -off).astype(BF16)
        y = dot(wf_ref[...], r0[b])
        wide = EDGE * TILE
        v = sum(y[a * ch : (a + 1) * ch, a * TILE : a * TILE + wide] for a in range(3))
        s = sigmoid(v)
        slope0[b] = s * (1.0 + v * (1.0 - s))
        h = (v * s).astype(BF16)
        flat = jnp.concatenate(
            [dot_t(h[:, 2 * TILE * t : 2 * TILE * (t + 1)], e0c).astype(BF16) for t in range(4)],
            axis=1,
        )
        to_patches(flat, p2, b)

    coarse_pre = dot(wd_ref[...], p2[...])
    s = sigmoid(coarse_pre)
    slope_down = s * (1.0 + coarse_pre * (1.0 - s))
    hidden1 = (coarse_pre * s).astype(BF16)
    h1[...] = hidden1
    second = [remote(h1, h1_lo, 4, up), remote(h1, h1_hi, 5, down)]

    lane = lax.broadcasted_iota(jnp.int32, (ch, TILE), 1)
    left = lane < cells
    nothing = jnp.zeros((ch, TILE), F32)

    def candidates(value, table, base):
        for b in range(nb):
            x = value[:, (b // 2) * TILE : (b // 2 + 1) * TILE].astype(F32)
            swapped = pltpu.roll(x, cells, axis=1)
            on_left, on_right = (x, swapped) if b % 2 == 0 else (swapped, x)
            cand[table, 0, base + b] = jnp.where(left, on_left, nothing).astype(BF16)
            cand[table, 1, base + b] = jnp.where(left, nothing, on_right).astype(BF16)

    for table in range(3):
        candidates(hidden1, table, 0)
        for half in range(2):
            cand[table, half, none] = nothing.astype(BF16)
            if table == 1:
                for n in range(nb, 2 * nb):
                    cand[table, half, n] = nothing.astype(BF16)
    up_back = dot(wu_ref[...], c2[...])
    for copy in second:
        copy.wait()
    candidates(h1_lo[...], 0, nb)
    candidates(h1_hi[...], 2, nb)

    q0 = q0_ref[...]
    top = (HALF - 1) * TILE

    def sources(b, i):
        parts = []
        for t in range(5):
            x = cand[i, 0, idx[b, 9 * i + 2 * t]]
            if t < 4:
                x = x + cand[i, 1, idx[b, 9 * i + 2 * t + 1]]
            parts.append(x)
        return jnp.concatenate(parts, axis=1)

    pairs = nb // 2
    wide1 = HALF * TILE
    gated = []
    delta_up = []
    for p in range(pairs):
        pads = []
        for b in (2 * p, 2 * p + 1):
            pads.append(
                jnp.concatenate(
                    [
                        dot(sources(b, 0), q0[:, top:]),
                        dot(sources(b, 1), q0),
                        dot(sources(b, 2), q0[:, :TILE]),
                    ],
                    axis=1,
                )
            )
        pad = pads[0] + turn(pads[1], cells)
        for n in range(9):
            off = (HALF + 2) * (n // 3 - 1) + n % 3 - 1
            r1[p, n * ch : (n + 1) * ch, :] = turn(pad, -off).astype(BF16)
        y = dot(wc_ref[...], r1[p])
        v = sum(y[a * ch : (a + 1) * ch, a * TILE : a * TILE + wide1] for a in range(3))
        s = sigmoid(v)
        slope = s * (1.0 + v * (1.0 - s))
        gated.append(dot_t((v * s).astype(BF16), q2_ref[...]).astype(BF16))
        ub = split_dot(dot, up_back[:, p * TILE : (p + 1) * TILE], q2_ref[...])
        delta = (ub * slope).astype(BF16)
        delta_up.append(delta)
        turned = []
        for n in range(9):
            off = (HALF + 2) * (n // 3 - 1) + n % 3 - 1
            turned.append(turn(delta.astype(F32), off).astype(BF16))
        y = dot(wct_ref[...], jnp.concatenate(turned, axis=0))
        gap = jnp.zeros((ch, TILE), F32)
        back = (
            jnp.concatenate([y[:ch], gap, gap], axis=1)
            + jnp.concatenate([gap, y[ch : 2 * ch], gap], axis=1)
            + jnp.concatenate([gap, gap, y[2 * ch :]], axis=1)
        )
        rim[0, p] = back[:, :TILE].astype(BF16)
        rim[1, p] = back[:, -TILE:].astype(BF16)
        for h in range(2):
            b = 2 * p + h
            x = turn(back, -h * cells)
            dg0[b] = split_dot(dot_t, x[:, TILE : TILE + wide1], q0)
            dgm[b] = split_dot(dot_t, x[:, :TILE], q0[:, top:])
            dgp[b] = split_dot(dot_t, x[:, -TILE:], q0[:, :TILE])
    third = [remote(rim.at[0], rim_hi, 6, down), remote(rim.at[1], rim_lo, 7, up)]

    gated = jnp.concatenate(gated, axis=1)
    dec = (p2[...].astype(F32) + dot(wut_ref[...], gated)).astype(BF16)

    def from_patches(value, b):
        return jnp.concatenate(
            [value[n * ch : (n + 1) * ch, b * cells : (b + 1) * cells] for n in range(8)], axis=1
        )

    for b in range(nb):
        out_ref[b] = dot_t(from_patches(dec, b), pm_ref[...]).astype(BF16)
    taps = 9 * ch
    grad_coarse = sum(dot_t(placed(delta_up[p], HALF), r1[p]) for p in range(pairs))
    for a in range(3):
        second_grads[:, a * taps : (a + 1) * taps] = grad_coarse[a * ch : (a + 1) * ch]
    held = 3 * taps + 8 * ch
    second_grads[:, 3 * taps : held] = dot_t(gated, c2[...])
    for ref in (first_grads, second_grads):
        ref[:, held:] = jnp.zeros((ch, ref.shape[1] - held), F32)
    second_sum.begin()

    dg0[nb] = jnp.zeros(dg0.shape[1:], F32)
    dgm[none] = jnp.zeros(dg0.shape[1:], F32)
    dgp[none] = jnp.zeros(dg0.shape[1:], F32)
    for copy in third:
        copy.wait()
    second_sum.scatter()
    for p in range(pairs):
        for h in range(2):
            x = turn(rim_hi[p].astype(F32), -h * cells).astype(BF16)
            dgm[nb + 2 * p + h] = dot_t(x, q0[:, top:])
            x = turn(rim_lo[p].astype(F32), -h * cells).astype(BF16)
            dgp[nb + 2 * p + h] = dot_t(x, q0[:, :TILE])
    for b in range(nb):
        sums = [nothing, nothing]
        for k in range(27):
            chunk = 8 - k % 9
            table = (dgp, dg0, dgm)[k // 9]
            t = chunk // 2
            sums[chunk % 2] = sums[chunk % 2] + table[idx[b, k], :, t * TILE : (t + 1) * TILE]
        gh1[:, b * cells : (b + 1) * cells] = sums[0][:, :cells] + sums[1][:, cells:]
    delta_down = (gh1[...] * slope_down).astype(BF16)
    first_grads[:, 3 * taps : held] = dot_t(delta_down, p2[...])
    gh0[...] = c2[...].astype(F32) + dot(wdt_ref[...], delta_down)
    grad_fine = jnp.zeros((3 * ch, taps), F32)
    for b in range(nb):
        flat = dot_t(from_patches(gh0[...], b).astype(BF16), pm_ref[...]).astype(BF16)
        wide_grad = jnp.concatenate([dot(t, e0c) for t in tiles(flat)], axis=1)
        delta = (wide_grad * slope0[b]).astype(BF16)
        grad_fine = grad_fine + dot_t(placed(delta, EDGE), r0[b])
    for a in range(3):
        first_grads[:, a * taps : (a + 1) * taps] = grad_fine[a * ch : (a + 1) * ch]
    first_sum.begin()
    second_sum.gather()
    first_sum.scatter()
    second_sum.finish(second_ref)
    first_sum.gather()
    first_sum.finish(first_ref)


def shards(features, neighbours, send_list, w_fine, w_down, w_coarse, w_up, cotangent):
    nb, ch = features.shape[1], features.shape[2]
    cols = nb * HALF**3
    peers = lax.axis_size("space")
    taps = 9 * ch

    def stacked(w):
        return w.reshape(ch, 3, taps).transpose(1, 0, 2).reshape(3 * ch, taps)

    wct = w_coarse.reshape(ch, 3, 9, ch).transpose(1, 3, 2, 0).reshape(3 * ch, taps)
    consts = [jnp.asarray(t(), BF16) for t in (fine_spread, coarse_spread, pair_spread, patch_order)]
    vmem = pl.BlockSpec(memory_space=pltpu.VMEM)
    smem = pl.BlockSpec(memory_space=pltpu.SMEM)
    v = pltpu.VMEM
    width = 10 * HALF**3
    factor = 1.0 / math.sqrt(lax.axis_size("rep") * peers * nb * EDGE**3)
    count = 3 * taps + 8 * ch
    share = group_width(count, peers)
    sums = [
        v((ch, peers // 2 * share), F32),
        v((2 * peers, 16, share), BF16),
        v((peers, 16, share), BF16),
        v((peers, 16, share), BF16),
        v((peers, 16, share), BF16),
        v((2 * peers, 16, share), BF16),
        pltpu.SemaphoreType.DMA((3 * peers,)),
        pltpu.SemaphoreType.DMA((3 * peers,)),
    ]
    decoded, second, first = pl.pallas_call(
        functools.partial(body, peers, factor),
        out_shape=(
            jax.ShapeDtypeStruct(features.shape[1:], BF16),
            jax.ShapeDtypeStruct((ch, count), F32),
            jax.ShapeDtypeStruct((ch, count), F32),
        ),
        in_specs=[vmem, smem] + [vmem] * 13,
        out_specs=(vmem, vmem, vmem),
        scratch_shapes=[
            v((nb + 1, ch, EDGE**3), BF16),
            v((2 * nb + 1, ch, TILE), BF16),
            v((2 * nb + 1, ch, TILE), BF16),
            v(send_list.shape[2:], jnp.int32),
            v(send_list.shape[2:], jnp.int32),
            pltpu.SMEM(send_list.shape[2:], jnp.int32),
            pltpu.SMEM(send_list.shape[2:], jnp.int32),
            pltpu.SMEM((nb, 27), jnp.int32),
            v((nb, taps, (EDGE + 2) * TILE), BF16),
            v((nb, ch, EDGE * TILE), F32),
            v((8 * ch, cols), BF16),
            v((8 * ch, cols), BF16),
            v((ch, cols), BF16),
            v((ch, cols), BF16),
            v((ch, cols), BF16),
            v((3, 2, 2 * nb + 1, ch, TILE), BF16),
            v((nb // 2, taps, (HALF + 2) * TILE), BF16),
            v((2, nb // 2, ch, TILE), BF16),
            v((nb // 2, ch, TILE), BF16),
            v((nb // 2, ch, TILE), BF16),
            v((nb + 1, ch, width), F32),
            v((2 * nb + 1, ch, width), F32),
            v((2 * nb + 1, ch, width), F32),
            v((ch, cols), F32),
            v((8 * ch, cols), F32),
            pltpu.SemaphoreType.DMA((8,)),
            pltpu.SemaphoreType.DMA((8,)),
            pltpu.SemaphoreType.DMA((2,)),
            *sums,
            *sums,
        ],
        compiler_params=pltpu.CompilerParams(
            collective_id=0, has_side_effects=True, vmem_limit_bytes=56 * 1024 * 1024
        ),
    )(
        features[0], neighbours[0], send_list[0, 0], cotangent[0],
        stacked(w_fine), w_down, stacked(w_coarse), wct, w_up, w_down.T, w_up.T, *consts,
    )
    cut = 3 * taps
    return decoded[None], first[:, :cut], first[:, cut:], second[:, :cut], second[:, cut:]


def solution(mesh):
    in_specs = (
        P("rep", "space", None, None),
        P("rep", "space", None),
        P("rep", "space", None, None),
        P(),
        P(),
        P(),
        P(),
        P("rep", "space", None, None),
    )
    out_specs = (P("rep", "space", None, None), P(), P(), P(), P())
    return jax.shard_map(shards, mesh=mesh, in_specs=in_specs, out_specs=out_specs, check_vma=False)
```

```python
import functools
import math

import jax
import jax.numpy as jnp
import numpy as np
from jax import lax
from jax.experimental import pallas as pl
from jax.experimental.pallas import tpu as pltpu
from jax.sharding import PartitionSpec as P

EDGE = 8
HALF = EDGE // 2
TILE = 128
F32 = jnp.float32
BF16 = jnp.bfloat16
MESH = pl.DeviceIdType.MESH


def spots(step, side):
    if step < 0:
        return [(side - 1, 0)]
    if step == 0:
        return [(v, v + 1) for v in range(side)]
    return [(0, side + 1)]


def fine_spread():
    table = np.zeros((9, 2, EDGE, EDGE, 2, TILE), np.float32)
    for j in (-1, 0, 1):
        for l in (-1, 0, 1):
            for y, py in spots(j, EDGE):
                for z, pz in spots(l, EDGE):
                    for x in range(2):
                        table[3 * (j + 1) + l + 1, x, y, z, x, (EDGE + 2) * py + pz] = 1
    return table.reshape(9 * 2 * EDGE * EDGE, 2 * TILE)


def coarse_spread():
    table = np.zeros((10, HALF, HALF, HALF, HALF, TILE), np.float32)
    for j in (-1, 0, 1):
        for l in (-1, 0, 1):
            for y, py in spots(j, HALF):
                for z, pz in spots(l, HALF):
                    for x in range(HALF):
                        table[3 * (j + 1) + l + 1, x, y, z, x, (HALF + 2) * py + pz] = 1
    return table.reshape(10 * HALF**3, HALF * TILE)


def pair_spread():
    centre = coarse_spread().reshape(10, HALF**3, HALF, TILE)[4]
    return np.concatenate([centre, np.roll(centre, 64, axis=-1)]).reshape(2 * HALF**3, HALF * TILE)


def patch_order():
    table = np.zeros((EDGE**3, EDGE**3), np.float32)
    for x in range(EDGE):
        for y in range(EDGE):
            for z in range(EDGE):
                part = 4 * (x % 2) + 2 * (y % 2) + z % 2
                cell = (x // 2 * HALF + y // 2) * HALF + z // 2
                table[(x * EDGE + y) * EDGE + z, part * HALF**3 + cell] = 1
    return table


def dot(a, b):
    return jnp.dot(a, b, preferred_element_type=F32)


def dot_t(a, b):
    return lax.dot_general(a, b, (((1,), (1,)), ((), ())), preferred_element_type=F32)


def split_dot(f, a, b):
    high = a.astype(BF16)
    low = (a - high.astype(F32)).astype(BF16)
    return f(high, b) + f(low, b)


def tiles(x):
    return [x[:, TILE * t : TILE * (t + 1)] for t in range(x.shape[1] // TILE)]


def turn(x, shift):
    shift = shift % TILE
    if shift == 0:
        return x
    return jnp.concatenate([pltpu.roll(t, shift, axis=1) for t in tiles(x)], axis=1)


def sigmoid(v):
    return 1.0 / (1.0 + jnp.exp(-v))


def placed(x, tile_count):
    rows = []
    for a in range(3):
        parts = []
        if a:
            parts.append(jnp.zeros((x.shape[0], a * TILE), x.dtype))
        parts.append(x)
        if a < 2:
            parts.append(jnp.zeros((x.shape[0], (2 - a) * TILE), x.dtype))
        rows.append(jnp.concatenate(parts, axis=1))
    return jnp.concatenate(rows, axis=0)


def group_width(count, peers):
    groups = peers // 2
    return -(-count // (groups * TILE)) * TILE


class Sum:
    def __init__(self, peers, factor, grads, part, pair, mid, got, full, send, recv):
        self.peers, self.factor = peers, factor
        self.grads, self.part, self.pair, self.mid, self.got, self.full = grads, part, pair, mid, got, full
        self.send, self.recv = send, recv
        self.me, self.rep = lax.axis_index("space"), lax.axis_index("rep")
        self.groups = peers // 2
        self.width = part.shape[2]

    def copy(self, src, dst, n, chip, core):
        return pltpu.make_async_remote_copy(
            src_ref=src, dst_ref=dst, send_sem=self.send.at[n], recv_sem=self.recv.at[n],
            device_id=(chip, core), device_id_type=MESH,
        )

    def pair_copy(self):
        other = 1 - self.rep
        src = self.part.at[pl.ds(other * self.peers, self.peers)]
        return self.copy(src, self.pair, 0, self.me, other)

    def share_copy(self, o):
        chip = lax.rem(self.me + o, self.peers)
        return self.copy(self.mid.at[chip], self.got.at[o], o, chip, self.rep)

    def total_copy(self, o, owner):
        chip = lax.rem(self.me + o, self.peers)
        spot = self.full.at[self.rep * self.peers + owner]
        return self.copy(spot, spot, self.peers + o, chip, self.rep)

    def core_copy(self, o):
        owner = lax.rem(self.me + self.peers - o, self.peers)
        spot = self.full.at[self.rep * self.peers + owner]
        return self.copy(spot, spot, 2 * self.peers + o, self.me, 1 - self.rep)

    def each(self, start, act):
        lax.fori_loop(start, self.peers, lambda o, c: (act(o), c)[1], 0)

    def begin(self):
        w = self.width
        for row in range(4):
            for col in range(self.groups):
                self.part[row * self.groups + col] = self.grads[
                    16 * row : 16 * row + 16, col * w : (col + 1) * w
                ].astype(BF16)
        self.pair_copy().start()

    def scatter(self):
        self.pair_copy().wait()
        mine = self.part[pl.ds(self.rep * self.peers, self.peers)]
        self.mid[...] = (mine.astype(F32) + self.pair[...].astype(F32)).astype(BF16)
        self.each(1, lambda o: self.share_copy(o).start())

    def gather(self):
        self.each(1, lambda o: self.share_copy(o).wait())
        total = self.mid[self.me].astype(F32)
        for o in range(1, self.peers):
            total = total + self.got[o].astype(F32)
        self.full[self.rep * self.peers + self.me] = (total * self.factor).astype(BF16)
        self.core_copy(0).start()
        self.each(1, lambda o: self.total_copy(o, self.me).start())

    def finish(self, outs):
        def pass_on(o):
            owner = lax.rem(self.me + self.peers - o, self.peers)
            self.total_copy(o, owner).wait_recv()
            self.core_copy(o).start()

        self.each(1, pass_on)
        self.each(1, lambda o: self.total_copy(o, self.me).wait_send())
        self.each(0, lambda o: self.core_copy(o).wait())
        per = self.width // TILE
        tile = 0
        for out in outs:
            for start in range(0, out.shape[1], TILE):
                size = min(TILE, out.shape[1] - start)
                inner = tile % per * TILE
                for row in range(4):
                    out[16 * row : 16 * row + 16, start : start + size] = self.full[
                        row * self.groups + tile // per, :, inner : inner + size
                    ].astype(F32)
                tile += 1


def body(
    peers, factor,
    f_ref, nb_ref, sl_ref, cot_ref, w_fine, wd_ref, w_coarse, wu_ref,
    e0_ref, q0_ref, q2_ref, pm_ref,
    out_ref, grad_fine_ref, grad_down_ref, grad_coarse_ref, grad_up_ref,
    wf_ref, wc_ref, wct_ref, a0,
    x0, fh, fl, sl_lo, sl_hi, sm_lo, sm_hi, idx, r0, slope0, p2, c2, h1, h1_lo, h1_hi,
    cand, r1, rim, rim_lo, rim_hi, dg0, dgm, dgp, gh1, gh0,
    send_sem, recv_sem, local_sem,
    *sums,
):
    second_sum = Sum(peers, factor, *sums[:8])
    first_sum = Sum(peers, factor, *sums[8:])
    second_grads, first_grads = second_sum.grads, first_sum.grads
    nb, ch = f_ref.shape[0], f_ref.shape[1]
    cells = HALF**3
    me = lax.axis_index("space")
    rep = lax.axis_index("rep")
    up = lax.rem(me + 1, peers)
    down = lax.rem(me + peers - 1, peers)

    barrier = pltpu.get_barrier_semaphore()

    def greet(o, carry):
        other = lax.rem(me + o, peers)
        pl.semaphore_signal(barrier, inc=1, device_id=(other, rep), device_id_type=MESH)
        return carry

    lax.fori_loop(1, peers, greet, 0)
    pl.semaphore_signal(barrier, inc=1, device_id=(me, 1 - rep), device_id_type=MESH)
    pl.semaphore_wait(barrier, peers)

    def remote(src, dst, n, other):
        copy = pltpu.make_async_remote_copy(
            src_ref=src, dst_ref=dst, send_sem=send_sem.at[n], recv_sem=recv_sem.at[n],
            device_id=(other, rep), device_id_type=MESH,
        )
        copy.start()
        return copy

    last = f_ref.shape[2] - TILE
    first = [
        remote(sl_ref, sl_lo, 0, up),
        remote(sl_ref, sl_hi, 1, down),
        remote(f_ref.at[:, :, last:], fh.at[nb : 2 * nb], 2, up),
        remote(f_ref.at[:, :, :TILE], fl.at[nb : 2 * nb], 3, down),
    ]

    x0[:nb] = f_ref[...]
    x0[nb] = jnp.zeros(x0.shape[1:], BF16)
    fh[:nb] = f_ref[:, :, last:]
    fl[:nb] = f_ref[:, :, :TILE]
    fh[2 * nb] = jnp.zeros(fh.shape[1:], BF16)
    fl[2 * nb] = jnp.zeros(fl.shape[1:], BF16)

    def to_patches(src, dst):
        moved = dot(src, pm_ref[...]).astype(BF16)
        for b in range(nb):
            for part in range(8):
                dst[part * ch : (part + 1) * ch, b * cells : (b + 1) * cells] = moved[
                    b * ch : (b + 1) * ch, part * cells : (part + 1) * cells
                ]

    def by_block(value):
        return [value[b * ch : (b + 1) * ch] for b in range(nb)]

    taps = 9 * ch
    for a in range(3):
        wf_ref[a * ch : (a + 1) * ch, :] = w_fine[:, a * taps : (a + 1) * taps]
        wc_ref[a * ch : (a + 1) * ch, :] = w_coarse[:, a * taps : (a + 1) * taps]
    for n in range(0, 27, 2):
        size = min(2, 27 - n)
        flipped = w_coarse[:, n * ch : (n + size) * ch].astype(F32).T.astype(BF16)
        for m in range(size):
            a, k = (n + m) // 9, (n + m) % 9
            wct_ref[a * ch : (a + 1) * ch, k * ch : (k + 1) * ch] = flipped[m * ch : (m + 1) * ch]
    wdt = wd_ref[...].astype(F32).T.astype(BF16)
    wut = wu_ref[...].astype(F32).T.astype(BF16)
    to_patches(jnp.concatenate([cot_ref[b] for b in range(nb)], axis=0), c2)

    first[0].wait()
    first[1].wait()
    to_smem = [
        pltpu.make_async_copy(sl_lo, sm_lo, local_sem.at[0]),
        pltpu.make_async_copy(sl_hi, sm_hi, local_sem.at[1]),
    ]
    for copy in to_smem:
        copy.start()
    for copy in to_smem:
        copy.wait()
    slots = sl_ref.shape[1]
    none = 2 * nb
    for b in range(nb):
        for k in range(27):
            if k == 13:
                idx[b, k] = jnp.int32(b)
                continue
            v = nb_ref[b, k if k < 13 else k - 1]
            if k < 9:
                far = nb + sm_lo[0, jnp.clip(v - nb, 0, slots - 1)]
                v = jnp.where(v < 0, none, jnp.where(v < nb, v, far))
            elif k >= 18:
                far = nb + sm_hi[1, jnp.clip(v - nb - slots, 0, slots - 1)]
                v = jnp.where(v < 0, none, jnp.where(v < nb, v, far))
            else:
                v = jnp.where(v < 0, nb, v)
            idx[b, k] = v
    first[2].wait()
    first[3].wait()

    e0 = e0_ref[...]
    e0c = e0_ref[4 * TILE : 5 * TILE, :]
    for b in range(nb):
        for n in range(9):
            for t in range(4):
                row = (4 * b + t) * ch
                a0[row : row + ch, n * TILE : (n + 1) * TILE] = x0[
                    idx[b, 9 + n], :, t * TILE : (t + 1) * TILE
                ]
    inner = dot(a0[...], e0)

    def faces(table, i):
        return jnp.concatenate(
            [
                jnp.concatenate([table[idx[b, 9 * i + n]] for n in range(9)], axis=1)
                for b in range(nb)
            ],
            axis=0,
        )

    low = by_block(dot(faces(fh, 0), e0[:, TILE:]))
    high = by_block(dot(faces(fl, 2), e0[:, :TILE]))
    wide = EDGE * TILE
    hidden0 = []
    for b in range(nb):
        middle = [inner[(4 * b + t) * ch : (4 * b + t + 1) * ch] for t in range(4)]
        pad = jnp.concatenate([low[b]] + middle + [high[b]], axis=1)
        for n in range(9):
            off = (EDGE + 2) * (n // 3 - 1) + n % 3 - 1
            r0[b, n * ch : (n + 1) * ch, :] = turn(pad, -off).astype(BF16)
        y = dot(wf_ref[...], r0[b])
        v = sum(y[a * ch : (a + 1) * ch, a * TILE : a * TILE + wide] for a in range(3))
        s = sigmoid(v)
        slope0[b] = s * (1.0 + v * (1.0 - s))
        h = (v * s).astype(BF16)
        hidden0 += [h[:, 2 * TILE * t : 2 * TILE * (t + 1)] for t in range(4)]
    flat = dot_t(jnp.concatenate(hidden0, axis=0), e0c).astype(BF16)

    def rows_to_lanes(value):
        return jnp.concatenate(
            [
                jnp.concatenate(
                    [value[(4 * b + t) * ch : (4 * b + t + 1) * ch] for t in range(4)], axis=1
                )
                for b in range(nb)
            ],
            axis=0,
        )

    to_patches(rows_to_lanes(flat), p2)

    coarse_pre = dot(wd_ref[...], p2[...])
    s = sigmoid(coarse_pre)
    slope_down = s * (1.0 + coarse_pre * (1.0 - s))
    hidden1 = (coarse_pre * s).astype(BF16)
    h1[...] = hidden1
    second = [remote(h1, h1_lo, 4, up), remote(h1, h1_hi, 5, down)]

    lane = lax.broadcasted_iota(jnp.int32, (ch, TILE), 1)
    left = lane < cells
    nothing = jnp.zeros((ch, TILE), F32)

    def candidates(value, table, base):
        for b in range(nb):
            x = value[:, (b // 2) * TILE : (b // 2 + 1) * TILE].astype(F32)
            swapped = pltpu.roll(x, cells, axis=1)
            on_left, on_right = (x, swapped) if b % 2 == 0 else (swapped, x)
            cand[table, 0, base + b] = jnp.where(left, on_left, nothing).astype(BF16)
            cand[table, 1, base + b] = jnp.where(left, nothing, on_right).astype(BF16)

    for table in range(3):
        candidates(hidden1, table, 0)
        for half in range(2):
            cand[table, half, none] = nothing.astype(BF16)
            if table == 1:
                for n in range(nb, 2 * nb):
                    cand[table, half, n] = nothing.astype(BF16)
    up_back = dot(wu_ref[...], c2[...])
    for copy in second:
        copy.wait()
    candidates(h1_lo[...], 0, nb)
    candidates(h1_hi[...], 2, nb)

    q0 = q0_ref[...]
    top = (HALF - 1) * TILE

    def sources(i):
        rows = []
        for b in range(nb):
            parts = []
            for t in range(5):
                x = cand[i, 0, idx[b, 9 * i + 2 * t]]
                if t < 4:
                    x = x + cand[i, 1, idx[b, 9 * i + 2 * t + 1]]
                parts.append(x)
            rows.append(jnp.concatenate(parts, axis=1))
        return jnp.concatenate(rows, axis=0)

    pairs = nb // 2
    wide1 = HALF * TILE
    pads = by_block(
        jnp.concatenate(
            [dot(sources(0), q0[:, top:]), dot(sources(1), q0), dot(sources(2), q0[:, :TILE])],
            axis=1,
        )
    )
    pre, ups = [], []
    for p in range(pairs):
        pad = pads[2 * p] + turn(pads[2 * p + 1], cells)
        for n in range(9):
            off = (HALF + 2) * (n // 3 - 1) + n % 3 - 1
            r1[p, n * ch : (n + 1) * ch, :] = turn(pad, -off).astype(BF16)
        y = dot(wc_ref[...], r1[p])
        pre.append(sum(y[a * ch : (a + 1) * ch, a * TILE : a * TILE + wide1] for a in range(3)))
        ups.append(up_back[:, p * TILE : (p + 1) * TILE])
    v = jnp.concatenate(pre, axis=0)
    s = sigmoid(v)
    slope = s * (1.0 + v * (1.0 - s))
    gated = dot_t((v * s).astype(BF16), q2_ref[...]).astype(BF16)
    delta = (split_dot(dot, jnp.concatenate(ups, axis=0), q2_ref[...]) * slope).astype(BF16)
    delta_up = [delta[p * ch : (p + 1) * ch] for p in range(pairs)]
    gated = jnp.concatenate([gated[p * ch : (p + 1) * ch] for p in range(pairs)], axis=1)
    gap = jnp.zeros((ch, TILE), F32)
    backs = []
    for p in range(pairs):
        turned = []
        for n in range(9):
            off = (HALF + 2) * (n // 3 - 1) + n % 3 - 1
            turned.append(turn(delta_up[p].astype(F32), off).astype(BF16))
        y = dot(wct_ref[...], jnp.concatenate(turned, axis=0))
        back = (
            jnp.concatenate([y[:ch], gap, gap], axis=1)
            + jnp.concatenate([gap, y[ch : 2 * ch], gap], axis=1)
            + jnp.concatenate([gap, gap, y[2 * ch :]], axis=1)
        )
        rim[0, p] = back[:, :TILE].astype(BF16)
        rim[1, p] = back[:, -TILE:].astype(BF16)
        backs += [back, turn(back, -cells)]
    third = [remote(rim.at[0], rim_hi, 6, down), remote(rim.at[1], rim_lo, 7, up)]

    backs = jnp.concatenate(backs, axis=0)
    for table, value, spread in (
        (dg0, backs[:, TILE : TILE + wide1], q0),
        (dgm, backs[:, :TILE], q0[:, top:]),
        (dgp, backs[:, -TILE:], q0[:, :TILE]),
    ):
        for b, x in enumerate(by_block(split_dot(dot_t, value, spread))):
            table[b] = x

    dec = (p2[...].astype(F32) + dot(wut, gated)).astype(BF16)

    def from_patches(value):
        return jnp.concatenate(
            [
                jnp.concatenate(
                    [
                        value[n * ch : (n + 1) * ch, b * cells : (b + 1) * cells]
                        for n in range(8)
                    ],
                    axis=1,
                )
                for b in range(nb)
            ],
            axis=0,
        )

    for b, x in enumerate(by_block(dot_t(from_patches(dec), pm_ref[...]).astype(BF16))):
        out_ref[b] = x
    held = 8 * ch
    second_grads[:, :held] = dot_t(gated, c2[...])
    grad_coarse = sum(dot_t(placed(delta_up[p], HALF), r1[p]) for p in range(pairs))
    for a in range(3):
        start = 2 * held + a * taps
        second_grads[:, start : start + taps] = grad_coarse[a * ch : (a + 1) * ch]
    for ref, used in ((first_grads, 3 * taps), (second_grads, 3 * taps + 2 * held)):
        ref[:, used:] = jnp.zeros((ch, ref.shape[1] - used), F32)

    dg0[nb] = jnp.zeros(dg0.shape[1:], F32)
    dgm[none] = jnp.zeros(dg0.shape[1:], F32)
    dgp[none] = jnp.zeros(dg0.shape[1:], F32)
    for copy in third:
        copy.wait()
    for table, ref, spread in ((dgm, rim_hi, q0[:, top:]), (dgp, rim_lo, q0[:, :TILE])):
        rows = []
        for p in range(pairs):
            x = ref[p].astype(F32)
            rows += [x, turn(x, -cells)]
        rows = jnp.concatenate(rows, axis=0).astype(BF16)
        for b, x in enumerate(by_block(dot_t(rows, spread))):
            table[nb + b] = x
    for b in range(nb):
        sums = [nothing, nothing]
        for k in range(27):
            chunk = 8 - k % 9
            table = (dgp, dg0, dgm)[k // 9]
            t = chunk // 2
            sums[chunk % 2] = sums[chunk % 2] + table[idx[b, k], :, t * TILE : (t + 1) * TILE]
        gh1[:, b * cells : (b + 1) * cells] = sums[0][:, :cells] + sums[1][:, cells:]
    delta_down = (gh1[...] * slope_down).astype(BF16)
    second_grads[:, held : 2 * held] = dot_t(delta_down, p2[...])
    second_sum.begin()
    gh0[...] = c2[...].astype(F32) + dot(wdt, delta_down)
    flat = dot_t(from_patches(gh0[...]).astype(BF16), pm_ref[...]).astype(BF16)
    spread = jnp.concatenate(
        [flat[b * ch : (b + 1) * ch, t * TILE : (t + 1) * TILE] for b in range(nb) for t in range(4)],
        axis=0,
    )
    wide_grad = by_block(rows_to_lanes(dot(spread, e0c)))
    second_sum.scatter()
    grad_fine = jnp.zeros((3 * ch, taps), F32)
    for b in range(nb):
        delta = (wide_grad[b] * slope0[b]).astype(BF16)
        grad_fine = grad_fine + dot_t(placed(delta, EDGE), r0[b])
        if b == nb // 2:
            second_sum.gather()
    for a in range(3):
        first_grads[:, a * taps : (a + 1) * taps] = grad_fine[a * ch : (a + 1) * ch]
    first_sum.begin()
    first_sum.scatter()
    second_sum.finish([grad_up_ref, grad_down_ref, grad_coarse_ref])
    first_sum.gather()
    first_sum.finish([grad_fine_ref])


def shards(features, neighbours, send_list, w_fine, w_down, w_coarse, w_up, cotangent):
    nb, ch = features.shape[1], features.shape[2]
    cols = nb * HALF**3
    peers = lax.axis_size("space")
    taps = 9 * ch

    consts = [jnp.asarray(t(), BF16) for t in (fine_spread, coarse_spread, pair_spread, patch_order)]
    vmem = pl.BlockSpec(memory_space=pltpu.VMEM)
    smem = pl.BlockSpec(memory_space=pltpu.SMEM)
    v = pltpu.VMEM
    width = 10 * HALF**3
    factor = 1.0 / math.sqrt(lax.axis_size("rep") * peers * nb * EDGE**3)

    def sum_buffers(count):
        share = group_width(count, peers)
        return [
            v((ch, peers // 2 * share), F32),
            v((2 * peers, 16, share), BF16),
            v((peers, 16, share), BF16),
            v((peers, 16, share), BF16),
            v((peers, 16, share), BF16),
            v((2 * peers, 16, share), BF16),
            pltpu.SemaphoreType.DMA((3 * peers,)),
            pltpu.SemaphoreType.DMA((3 * peers,)),
        ]

    decoded, *grads = pl.pallas_call(
        functools.partial(body, peers, factor),
        out_shape=(
            jax.ShapeDtypeStruct(features.shape[1:], BF16),
            *[jax.ShapeDtypeStruct(w.shape, F32) for w in (w_fine, w_down, w_coarse, w_up)],
        ),
        in_specs=[vmem, smem] + [vmem] * 10,
        out_specs=(vmem,) * 5,
        scratch_shapes=[
            v((3 * ch, taps), BF16),
            v((3 * ch, taps), BF16),
            v((3 * ch, taps), BF16),
            v((4 * nb * ch, 9 * TILE), BF16),
            v((nb + 1, ch, EDGE**3), BF16),
            v((2 * nb + 1, ch, TILE), BF16),
            v((2 * nb + 1, ch, TILE), BF16),
            v(send_list.shape[2:], jnp.int32),
            v(send_list.shape[2:], jnp.int32),
            pltpu.SMEM(send_list.shape[2:], jnp.int32),
            pltpu.SMEM(send_list.shape[2:], jnp.int32),
            pltpu.SMEM((nb, 27), jnp.int32),
            v((nb, taps, (EDGE + 2) * TILE), BF16),
            v((nb, ch, EDGE * TILE), F32),
            v((8 * ch, cols), BF16),
            v((8 * ch, cols), BF16),
            v((ch, cols), BF16),
            v((ch, cols), BF16),
            v((ch, cols), BF16),
            v((3, 2, 2 * nb + 1, ch, TILE), BF16),
            v((nb // 2, taps, (HALF + 2) * TILE), BF16),
            v((2, nb // 2, ch, TILE), BF16),
            v((nb // 2, ch, TILE), BF16),
            v((nb // 2, ch, TILE), BF16),
            v((nb + 1, ch, width), F32),
            v((2 * nb + 1, ch, width), F32),
            v((2 * nb + 1, ch, width), F32),
            v((ch, cols), F32),
            v((8 * ch, cols), F32),
            pltpu.SemaphoreType.DMA((8,)),
            pltpu.SemaphoreType.DMA((8,)),
            pltpu.SemaphoreType.DMA((2,)),
            *sum_buffers(3 * taps + 16 * ch),
            *sum_buffers(3 * taps),
        ],
        compiler_params=pltpu.CompilerParams(
            collective_id=0, has_side_effects=True, vmem_limit_bytes=56 * 1024 * 1024
        ),
    )(
        features[0], neighbours[0], send_list[0, 0], cotangent[0],
        w_fine, w_down, w_coarse, w_up, *consts,
    )
    return decoded[None], *grads


def solution(mesh):
    in_specs = (
        P("rep", "space", None, None),
        P("rep", "space", None),
        P("rep", "space", None, None),
        P(),
        P(),
        P(),
        P(),
        P("rep", "space", None, None),
    )
    out_specs = (P("rep", "space", None, None), P(), P(), P(), P())
    return jax.shard_map(shards, mesh=mesh, in_specs=in_specs, out_specs=out_specs, check_vma=False)
```

```python
import functools
import math

import jax
import jax.numpy as jnp
import numpy as np
from jax import lax
from jax.experimental import pallas as pl
from jax.experimental.pallas import tpu as pltpu
from jax.sharding import PartitionSpec as P

EDGE = 8
HALF = EDGE // 2
TILE = 128
F32 = jnp.float32
BF16 = jnp.bfloat16
MESH = pl.DeviceIdType.MESH


def spots(step, side):
    if step < 0:
        return [(side - 1, 0)]
    if step == 0:
        return [(v, v + 1) for v in range(side)]
    return [(0, side + 1)]


def fine_spread():
    table = np.zeros((9, 2, EDGE, EDGE, 2, TILE), np.float32)
    for j in (-1, 0, 1):
        for l in (-1, 0, 1):
            for y, py in spots(j, EDGE):
                for z, pz in spots(l, EDGE):
                    for x in range(2):
                        table[3 * (j + 1) + l + 1, x, y, z, x, (EDGE + 2) * py + pz] = 1
    return table.reshape(9 * 2 * EDGE * EDGE, 2 * TILE)


def coarse_spread():
    table = np.zeros((10, HALF, HALF, HALF, HALF, TILE), np.float32)
    for j in (-1, 0, 1):
        for l in (-1, 0, 1):
            for y, py in spots(j, HALF):
                for z, pz in spots(l, HALF):
                    for x in range(HALF):
                        table[3 * (j + 1) + l + 1, x, y, z, x, (HALF + 2) * py + pz] = 1
    return table.reshape(10 * HALF**3, HALF * TILE)


def pair_spread():
    centre = coarse_spread().reshape(10, HALF**3, HALF, TILE)[4]
    return np.concatenate([centre, np.roll(centre, 64, axis=-1)]).reshape(2 * HALF**3, HALF * TILE)


def patch_order():
    table = np.zeros((EDGE**3, EDGE**3), np.float32)
    for x in range(EDGE):
        for y in range(EDGE):
            for z in range(EDGE):
                part = 4 * (x % 2) + 2 * (y % 2) + z % 2
                cell = (x // 2 * HALF + y // 2) * HALF + z // 2
                table[(x * EDGE + y) * EDGE + z, part * HALF**3 + cell] = 1
    return table


def dot(a, b):
    return jnp.dot(a, b, preferred_element_type=F32)


def dot_t(a, b):
    return lax.dot_general(a, b, (((1,), (1,)), ((), ())), preferred_element_type=F32)


def split_dot(f, a, b):
    high = a.astype(BF16)
    low = (a - high.astype(F32)).astype(BF16)
    return f(high, b) + f(low, b)


def tiles(x):
    return [x[:, TILE * t : TILE * (t + 1)] for t in range(x.shape[1] // TILE)]


def turn(x, shift):
    shift = shift % TILE
    if shift == 0:
        return x
    return jnp.concatenate([pltpu.roll(t, shift, axis=1) for t in tiles(x)], axis=1)


def sigmoid(v):
    return 1.0 / (1.0 + jnp.exp(-v))


def placed_rows(x):
    columns = []
    for a in range(3):
        parts = []
        if a:
            parts.append(jnp.zeros((a * TILE, x.shape[1]), x.dtype))
        parts.append(x)
        if a < 2:
            parts.append(jnp.zeros(((2 - a) * TILE, x.shape[1]), x.dtype))
        columns.append(jnp.concatenate(parts, axis=0))
    return jnp.concatenate(columns, axis=1)


def flipped(x):
    return jnp.concatenate(
        [x[:, t : min(t + TILE, x.shape[1])].T for t in range(0, x.shape[1], TILE)], axis=0
    )


def group_width(count, peers):
    groups = peers // 2
    return -(-count // (groups * TILE)) * TILE


class Sum:
    def __init__(self, peers, factor, grads, part, pair, mid, got, full, send, recv):
        self.peers, self.factor = peers, factor
        self.grads, self.part, self.pair, self.mid, self.got, self.full = grads, part, pair, mid, got, full
        self.send, self.recv = send, recv
        self.me, self.rep = lax.axis_index("space"), lax.axis_index("rep")
        self.groups = peers // 2
        self.width = part.shape[2]

    def copy(self, src, dst, n, chip, core):
        return pltpu.make_async_remote_copy(
            src_ref=src, dst_ref=dst, send_sem=self.send.at[n], recv_sem=self.recv.at[n],
            device_id=(chip, core), device_id_type=MESH,
        )

    def pair_copy(self):
        other = 1 - self.rep
        src = self.part.at[pl.ds(other * self.peers, self.peers)]
        return self.copy(src, self.pair, 0, self.me, other)

    def share_copy(self, o):
        chip = lax.rem(self.me + o, self.peers)
        return self.copy(self.mid.at[chip], self.got.at[o], o, chip, self.rep)

    def total_copy(self, o, owner):
        chip = lax.rem(self.me + o, self.peers)
        spot = self.full.at[self.rep * self.peers + owner]
        return self.copy(spot, spot, self.peers + o, chip, self.rep)

    def core_copy(self, o):
        owner = lax.rem(self.me + self.peers - o, self.peers)
        spot = self.full.at[self.rep * self.peers + owner]
        return self.copy(spot, spot, 2 * self.peers + o, self.me, 1 - self.rep)

    def each(self, start, act):
        lax.fori_loop(start, self.peers, lambda o, c: (act(o), c)[1], 0)

    def begin(self):
        w = self.width
        for row in range(4):
            for col in range(self.groups):
                self.part[row * self.groups + col] = self.grads[
                    16 * row : 16 * row + 16, col * w : (col + 1) * w
                ].astype(BF16)
        self.pair_copy().start()

    def scatter(self):
        self.pair_copy().wait()
        mine = self.part[pl.ds(self.rep * self.peers, self.peers)]
        self.mid[...] = (mine.astype(F32) + self.pair[...].astype(F32)).astype(BF16)
        self.each(1, lambda o: self.share_copy(o).start())

    def gather(self):
        self.each(1, lambda o: self.share_copy(o).wait())
        total = self.mid[self.me].astype(F32)
        for o in range(1, self.peers):
            total = total + self.got[o].astype(F32)
        self.full[self.rep * self.peers + self.me] = (total * self.factor).astype(BF16)
        self.core_copy(0).start()
        self.each(1, lambda o: self.total_copy(o, self.me).start())

    def finish(self, out):
        def pass_on(o):
            owner = lax.rem(self.me + self.peers - o, self.peers)
            self.total_copy(o, owner).wait_recv()
            self.core_copy(o).start()

        self.each(1, pass_on)
        self.each(1, lambda o: self.total_copy(o, self.me).wait_send())
        self.each(0, lambda o: self.core_copy(o).wait())
        out[...] = self.full[...]


def unpack(groups, dec_in, second, first, dec_out, fine, down, coarse, up, sem):
    copy = pltpu.make_async_copy(dec_in, dec_out, sem)
    copy.start()
    for full, outs in ((second, (up, down, coarse)), (first, (fine,))):
        per = full.shape[2] // TILE
        tile = 0
        for out in outs:
            for start in range(0, out.shape[1], TILE):
                size = min(TILE, out.shape[1] - start)
                inner = tile % per * TILE
                for row in range(4):
                    out[16 * row : 16 * row + 16, start : start + size] = full[
                        row * groups + tile // per, :, inner : inner + size
                    ].astype(F32)
                tile += 1
    copy.wait()


def body(
    peers, factor,
    f_ref, nb_ref, sl_ref, cot_ref, w_fine, wd_ref, w_coarse, wu_ref,
    e0_ref, q0_ref, q2_ref, pm_ref,
    out_ref, second_ref, first_ref,
    wf_ref, wc_ref, wct_ref, a0,
    x0, fh, fl, sl_lo, sl_hi, sm_lo, sm_hi, idx, r0, slope0, p2, c2, h1, h1_lo, h1_hi,
    cand, r1, rim, rim_lo, rim_hi, dg0, dgm, dgp, gh1, gh0,
    send_sem, recv_sem, local_sem,
    *sums,
):
    second_sum = Sum(peers, factor, *sums[:8])
    first_sum = Sum(peers, factor, *sums[8:])
    second_grads, first_grads = second_sum.grads, first_sum.grads
    nb, ch = f_ref.shape[0], f_ref.shape[1]
    cells = HALF**3
    me = lax.axis_index("space")
    rep = lax.axis_index("rep")
    up = lax.rem(me + 1, peers)
    down = lax.rem(me + peers - 1, peers)

    barrier = pltpu.get_barrier_semaphore()

    def greet(o, carry):
        other = lax.rem(me + o, peers)
        pl.semaphore_signal(barrier, inc=1, device_id=(other, rep), device_id_type=MESH)
        return carry

    lax.fori_loop(1, peers, greet, 0)
    pl.semaphore_signal(barrier, inc=1, device_id=(me, 1 - rep), device_id_type=MESH)
    pl.semaphore_wait(barrier, peers)

    def remote(src, dst, n, other):
        copy = pltpu.make_async_remote_copy(
            src_ref=src, dst_ref=dst, send_sem=send_sem.at[n], recv_sem=recv_sem.at[n],
            device_id=(other, rep), device_id_type=MESH,
        )
        copy.start()
        return copy

    last = f_ref.shape[2] - TILE
    first = [
        remote(sl_ref, sl_lo, 0, up),
        remote(sl_ref, sl_hi, 1, down),
        remote(f_ref.at[:, :, last:], fh.at[nb : 2 * nb], 2, up),
        remote(f_ref.at[:, :, :TILE], fl.at[nb : 2 * nb], 3, down),
    ]

    x0[:nb] = f_ref[...]
    x0[nb] = jnp.zeros(x0.shape[1:], BF16)
    fh[:nb] = f_ref[:, :, last:]
    fl[:nb] = f_ref[:, :, :TILE]
    fh[2 * nb] = jnp.zeros(fh.shape[1:], BF16)
    fl[2 * nb] = jnp.zeros(fl.shape[1:], BF16)

    def to_patches(src, dst):
        moved = dot(src, pm_ref[...]).astype(BF16)
        for b in range(nb):
            for part in range(8):
                dst[part * ch : (part + 1) * ch, b * cells : (b + 1) * cells] = moved[
                    b * ch : (b + 1) * ch, part * cells : (part + 1) * cells
                ]

    def by_block(value):
        return [value[b * ch : (b + 1) * ch] for b in range(nb)]

    taps = 9 * ch
    for a in range(3):
        wf_ref[a * ch : (a + 1) * ch, :] = w_fine[:, a * taps : (a + 1) * taps]
        wc_ref[a * ch : (a + 1) * ch, :] = w_coarse[:, a * taps : (a + 1) * taps]
    for n in range(0, 27, 2):
        size = min(2, 27 - n)
        turned = w_coarse[:, n * ch : (n + size) * ch].astype(F32).T.astype(BF16)
        for m in range(size):
            a, k = (n + m) // 9, (n + m) % 9
            wct_ref[a * ch : (a + 1) * ch, k * ch : (k + 1) * ch] = turned[m * ch : (m + 1) * ch]
    wdt = wd_ref[...].astype(F32).T.astype(BF16)
    wut = wu_ref[...].astype(F32).T.astype(BF16)
    to_patches(jnp.concatenate([cot_ref[b] for b in range(nb)], axis=0), c2)

    first[0].wait()
    first[1].wait()
    to_smem = [
        pltpu.make_async_copy(sl_lo, sm_lo, local_sem.at[0]),
        pltpu.make_async_copy(sl_hi, sm_hi, local_sem.at[1]),
    ]
    for copy in to_smem:
        copy.start()
    for copy in to_smem:
        copy.wait()
    slots = sl_ref.shape[1]
    none = 2 * nb
    for b in range(nb):
        for k in range(27):
            if k == 13:
                idx[b, k] = jnp.int32(b)
                continue
            v = nb_ref[b, k if k < 13 else k - 1]
            if k < 9:
                far = nb + sm_lo[0, jnp.clip(v - nb, 0, slots - 1)]
                v = jnp.where(v < 0, none, jnp.where(v < nb, v, far))
            elif k >= 18:
                far = nb + sm_hi[1, jnp.clip(v - nb - slots, 0, slots - 1)]
                v = jnp.where(v < 0, none, jnp.where(v < nb, v, far))
            else:
                v = jnp.where(v < 0, nb, v)
            idx[b, k] = v
    first[2].wait()
    first[3].wait()

    e0 = e0_ref[...]
    e0c = e0_ref[4 * TILE : 5 * TILE, :]
    for b in range(nb):
        for n in range(9):
            for t in range(4):
                row = (4 * b + t) * ch
                a0[row : row + ch, n * TILE : (n + 1) * TILE] = x0[
                    idx[b, 9 + n], :, t * TILE : (t + 1) * TILE
                ]
    inner = dot(a0[...], e0)

    def faces(table, i):
        return jnp.concatenate(
            [
                jnp.concatenate([table[idx[b, 9 * i + n]] for n in range(9)], axis=1)
                for b in range(nb)
            ],
            axis=0,
        )

    low = by_block(dot(faces(fh, 0), e0[:, TILE:]))
    high = by_block(dot(faces(fl, 2), e0[:, :TILE]))
    wide = EDGE * TILE
    span = wide + 2 * TILE
    hidden0 = []
    for b in range(nb):
        middle = [inner[(4 * b + t) * ch : (4 * b + t + 1) * ch] for t in range(4)]
        pad = jnp.concatenate([low[b]] + middle + [high[b]], axis=1)
        for n in range(9):
            off = (EDGE + 2) * (n // 3 - 1) + n % 3 - 1
            r0[n * ch : (n + 1) * ch, b * span : (b + 1) * span] = turn(pad, -off).astype(BF16)
        y = dot(wf_ref[...], r0[:, b * span : (b + 1) * span])
        v = sum(y[a * ch : (a + 1) * ch, a * TILE : a * TILE + wide] for a in range(3))
        s = sigmoid(v)
        slope0[b] = s * (1.0 + v * (1.0 - s))
        h = (v * s).astype(BF16)
        hidden0 += [h[:, 2 * TILE * t : 2 * TILE * (t + 1)] for t in range(4)]
    flat = dot_t(jnp.concatenate(hidden0, axis=0), e0c).astype(BF16)

    def rows_to_lanes(value):
        return jnp.concatenate(
            [
                jnp.concatenate(
                    [value[(4 * b + t) * ch : (4 * b + t + 1) * ch] for t in range(4)], axis=1
                )
                for b in range(nb)
            ],
            axis=0,
        )

    to_patches(rows_to_lanes(flat), p2)

    coarse_pre = dot(wd_ref[...], p2[...])
    s = sigmoid(coarse_pre)
    slope_down = s * (1.0 + coarse_pre * (1.0 - s))
    hidden1 = (coarse_pre * s).astype(BF16)
    h1[...] = hidden1
    second = [remote(h1, h1_lo, 4, up), remote(h1, h1_hi, 5, down)]

    lane = lax.broadcasted_iota(jnp.int32, (ch, TILE), 1)
    left = lane < cells
    nothing = jnp.zeros((ch, TILE), F32)

    def candidates(value, table, base):
        for b in range(nb):
            x = value[:, (b // 2) * TILE : (b // 2 + 1) * TILE].astype(F32)
            swapped = pltpu.roll(x, cells, axis=1)
            on_left, on_right = (x, swapped) if b % 2 == 0 else (swapped, x)
            cand[table, 0, base + b] = jnp.where(left, on_left, nothing).astype(BF16)
            cand[table, 1, base + b] = jnp.where(left, nothing, on_right).astype(BF16)

    for table in range(3):
        candidates(hidden1, table, 0)
        for half in range(2):
            cand[table, half, none] = nothing.astype(BF16)
            if table == 1:
                for n in range(nb, 2 * nb):
                    cand[table, half, n] = nothing.astype(BF16)
    up_back = dot(wu_ref[...], c2[...])
    q0 = q0_ref[...]
    top = (HALF - 1) * TILE

    def sources(i):
        rows = []
        for b in range(nb):
            parts = []
            for t in range(5):
                x = cand[i, 0, idx[b, 9 * i + 2 * t]]
                if t < 4:
                    x = x + cand[i, 1, idx[b, 9 * i + 2 * t + 1]]
                parts.append(x)
            rows.append(jnp.concatenate(parts, axis=1))
        return jnp.concatenate(rows, axis=0)

    pairs = nb // 2
    wide1 = HALF * TILE
    inner1 = dot(sources(1), q0)
    for copy in second:
        copy.wait()
    candidates(h1_lo[...], 0, nb)
    candidates(h1_hi[...], 2, nb)

    pads = by_block(
        jnp.concatenate(
            [dot(sources(0), q0[:, top:]), inner1, dot(sources(2), q0[:, :TILE])],
            axis=1,
        )
    )
    pre, ups = [], []
    for p in range(pairs):
        pad = pads[2 * p] + turn(pads[2 * p + 1], cells)
        for n in range(9):
            off = (HALF + 2) * (n // 3 - 1) + n % 3 - 1
            r1[p, n * ch : (n + 1) * ch, :] = turn(pad, -off).astype(BF16)
        y = dot(wc_ref[...], r1[p])
        pre.append(sum(y[a * ch : (a + 1) * ch, a * TILE : a * TILE + wide1] for a in range(3)))
        ups.append(up_back[:, p * TILE : (p + 1) * TILE])
    v = jnp.concatenate(pre, axis=0)
    s = sigmoid(v)
    slope = s * (1.0 + v * (1.0 - s))
    gated = dot_t((v * s).astype(BF16), q2_ref[...]).astype(BF16)
    delta = (split_dot(dot, jnp.concatenate(ups, axis=0), q2_ref[...]) * slope).astype(BF16)
    delta_up = [delta[p * ch : (p + 1) * ch] for p in range(pairs)]
    gated = jnp.concatenate([gated[p * ch : (p + 1) * ch] for p in range(pairs)], axis=1)
    gap = jnp.zeros((ch, TILE), F32)
    backs = []
    for p in range(pairs):
        turned = []
        for n in range(9):
            off = (HALF + 2) * (n // 3 - 1) + n % 3 - 1
            turned.append(turn(delta_up[p].astype(F32), off).astype(BF16))
        y = dot(wct_ref[...], jnp.concatenate(turned, axis=0))
        back = (
            jnp.concatenate([y[:ch], gap, gap], axis=1)
            + jnp.concatenate([gap, y[ch : 2 * ch], gap], axis=1)
            + jnp.concatenate([gap, gap, y[2 * ch :]], axis=1)
        )
        rim[0, p] = back[:, :TILE].astype(BF16)
        rim[1, p] = back[:, -TILE:].astype(BF16)
        backs += [back, turn(back, -cells)]
    third = [remote(rim.at[0], rim_hi, 6, down), remote(rim.at[1], rim_lo, 7, up)]

    backs = jnp.concatenate(backs, axis=0)
    for table, value, spread in (
        (dg0, backs[:, TILE : TILE + wide1], q0),
        (dgm, backs[:, :TILE], q0[:, top:]),
        (dgp, backs[:, -TILE:], q0[:, :TILE]),
    ):
        for b, x in enumerate(by_block(dot_t(value.astype(BF16), spread))):
            table[b] = x

    dec = (p2[...].astype(F32) + dot(wut, gated)).astype(BF16)

    def from_patches(value):
        return jnp.concatenate(
            [
                jnp.concatenate(
                    [
                        value[n * ch : (n + 1) * ch, b * cells : (b + 1) * cells]
                        for n in range(8)
                    ],
                    axis=1,
                )
                for b in range(nb)
            ],
            axis=0,
        )

    for b, x in enumerate(by_block(dot_t(from_patches(dec), pm_ref[...]).astype(BF16))):
        out_ref[b] = x
    held = 8 * ch
    second_grads[:, :held] = dot_t(gated, c2[...])
    grad_coarse = flipped(
        sum(dot(r1[p], placed_rows(delta_up[p].astype(F32).T.astype(BF16))) for p in range(pairs))
    )
    for a in range(3):
        start = 2 * held + a * taps
        second_grads[:, start : start + taps] = grad_coarse[a * ch : (a + 1) * ch]
    for ref, used in ((first_grads, 3 * taps), (second_grads, 3 * taps + 2 * held)):
        ref[:, used:] = jnp.zeros((ch, ref.shape[1] - used), F32)

    dg0[nb] = jnp.zeros(dg0.shape[1:], F32)
    dgm[none] = jnp.zeros(dg0.shape[1:], F32)
    dgp[none] = jnp.zeros(dg0.shape[1:], F32)
    for copy in third:
        copy.wait()
    for table, ref, spread in ((dgm, rim_hi, q0[:, top:]), (dgp, rim_lo, q0[:, :TILE])):
        rows = []
        for p in range(pairs):
            x = ref[p].astype(F32)
            rows += [x, turn(x, -cells)]
        rows = jnp.concatenate(rows, axis=0).astype(BF16)
        for b, x in enumerate(by_block(dot_t(rows, spread))):
            table[nb + b] = x
    for b in range(nb):
        sums = [nothing, nothing]
        for k in range(27):
            chunk = 8 - k % 9
            table = (dgp, dg0, dgm)[k // 9]
            t = chunk // 2
            sums[chunk % 2] = sums[chunk % 2] + table[idx[b, k], :, t * TILE : (t + 1) * TILE]
        gh1[:, b * cells : (b + 1) * cells] = sums[0][:, :cells] + sums[1][:, cells:]
    delta_down = (gh1[...] * slope_down).astype(BF16)
    second_grads[:, held : 2 * held] = dot_t(delta_down, p2[...])
    second_sum.begin()
    gh0[...] = c2[...].astype(F32) + dot(wdt, delta_down)
    flat = dot_t(from_patches(gh0[...]).astype(BF16), pm_ref[...]).astype(BF16)
    spread = jnp.concatenate(
        [flat[b * ch : (b + 1) * ch, t * TILE : (t + 1) * TILE] for b in range(nb) for t in range(4)],
        axis=0,
    )
    wide_grad = by_block(rows_to_lanes(dot(spread, e0c)))
    second_sum.scatter()
    grad_fine = []
    for half in range(2):
        blocks = range(half * nb // 2, (half + 1) * nb // 2)
        deltas = [placed_rows((wide_grad[b] * slope0[b]).T.astype(BF16)) for b in blocks]
        cols = r0[:, blocks.start * span : blocks.stop * span]
        grad_fine.append(dot(cols, jnp.concatenate(deltas, axis=0)))
        if half == 0:
            second_sum.gather()
    grad_fine = flipped(grad_fine[0] + grad_fine[1])
    for a in range(3):
        first_grads[:, a * taps : (a + 1) * taps] = grad_fine[a * ch : (a + 1) * ch]
    first_sum.begin()
    first_sum.scatter()
    second_sum.finish(second_ref)
    first_sum.gather()
    first_sum.finish(first_ref)


def shards(features, neighbours, send_list, w_fine, w_down, w_coarse, w_up, cotangent):
    nb, ch = features.shape[1], features.shape[2]
    cols = nb * HALF**3
    peers = lax.axis_size("space")
    taps = 9 * ch

    consts = [jnp.asarray(t(), BF16) for t in (fine_spread, coarse_spread, pair_spread, patch_order)]
    vmem = pl.BlockSpec(memory_space=pltpu.VMEM)
    smem = pl.BlockSpec(memory_space=pltpu.SMEM)
    v = pltpu.VMEM
    width = 10 * HALF**3
    factor = 1.0 / math.sqrt(lax.axis_size("rep") * peers * nb * EDGE**3)

    def sum_buffers(share):
        return [
            v((ch, peers // 2 * share), F32),
            v((2 * peers, 16, share), BF16),
            v((peers, 16, share), BF16),
            v((peers, 16, share), BF16),
            v((peers, 16, share), BF16),
            v((2 * peers, 16, share), BF16),
            pltpu.SemaphoreType.DMA((3 * peers,)),
            pltpu.SemaphoreType.DMA((3 * peers,)),
        ]

    shares = [group_width(n, peers) for n in (3 * taps + 16 * ch, 3 * taps)]
    half_done = pl.pallas_call(
        functools.partial(body, peers, factor),
        out_shape=(
            jax.ShapeDtypeStruct(features.shape[1:], BF16),
            *[jax.ShapeDtypeStruct((2 * peers, 16, share), BF16) for share in shares],
        ),
        in_specs=[vmem, smem] + [vmem] * 10,
        out_specs=(vmem,) * 3,
        scratch_shapes=[
            v((3 * ch, taps), BF16),
            v((3 * ch, taps), BF16),
            v((3 * ch, taps), BF16),
            v((4 * nb * ch, 9 * TILE), BF16),
            v((nb + 1, ch, EDGE**3), BF16),
            v((2 * nb + 1, ch, TILE), BF16),
            v((2 * nb + 1, ch, TILE), BF16),
            v(send_list.shape[2:], jnp.int32),
            v(send_list.shape[2:], jnp.int32),
            pltpu.SMEM(send_list.shape[2:], jnp.int32),
            pltpu.SMEM(send_list.shape[2:], jnp.int32),
            pltpu.SMEM((nb, 27), jnp.int32),
            v((taps, nb * (EDGE + 2) * TILE), BF16),
            v((nb, ch, EDGE * TILE), F32),
            v((8 * ch, cols), BF16),
            v((8 * ch, cols), BF16),
            v((ch, cols), BF16),
            v((ch, cols), BF16),
            v((ch, cols), BF16),
            v((3, 2, 2 * nb + 1, ch, TILE), BF16),
            v((nb // 2, taps, (HALF + 2) * TILE), BF16),
            v((2, nb // 2, ch, TILE), BF16),
            v((nb // 2, ch, TILE), BF16),
            v((nb // 2, ch, TILE), BF16),
            v((nb + 1, ch, width), F32),
            v((2 * nb + 1, ch, width), F32),
            v((2 * nb + 1, ch, width), F32),
            v((ch, cols), F32),
            v((8 * ch, cols), F32),
            pltpu.SemaphoreType.DMA((8,)),
            pltpu.SemaphoreType.DMA((8,)),
            pltpu.SemaphoreType.DMA((2,)),
            *sum_buffers(shares[0]),
            *sum_buffers(shares[1]),
        ],
        compiler_params=pltpu.CompilerParams(
            collective_id=0, has_side_effects=True, vmem_limit_bytes=56 * 1024 * 1024
        ),
    )(
        features[0], neighbours[0], send_list[0, 0], cotangent[0],
        w_fine, w_down, w_coarse, w_up, *consts,
    )
    anywhere = pl.BlockSpec(memory_space=pl.ANY)
    decoded, *grads = pl.pallas_call(
        functools.partial(unpack, peers // 2),
        out_shape=(
            jax.ShapeDtypeStruct(features.shape[1:], BF16),
            *[jax.ShapeDtypeStruct(w.shape, F32) for w in (w_fine, w_down, w_coarse, w_up)],
        ),
        in_specs=[anywhere, vmem, vmem],
        out_specs=(anywhere, vmem, vmem, vmem, vmem),
        scratch_shapes=[pltpu.SemaphoreType.DMA],
        compiler_params=pltpu.CompilerParams(vmem_limit_bytes=32 * 1024 * 1024),
    )(*half_done)
    return decoded[None], *grads


def solution(mesh):
    in_specs = (
        P("rep", "space", None, None),
        P("rep", "space", None),
        P("rep", "space", None, None),
        P(),
        P(),
        P(),
        P(),
        P("rep", "space", None, None),
    )
    out_specs = (P("rep", "space", None, None), P(), P(), P(), P())
    return jax.shard_map(shards, mesh=mesh, in_specs=in_specs, out_specs=out_specs, check_vma=False)
```

```python
import functools
import math

import jax
import jax.numpy as jnp
import numpy as np
from jax import lax
from jax.experimental import pallas as pl
from jax.experimental.pallas import tpu as pltpu
from jax.sharding import PartitionSpec as P

EDGE = 8
HALF = EDGE // 2
TILE = 128
F32 = jnp.float32
BF16 = jnp.bfloat16
MESH = pl.DeviceIdType.MESH


def spots(step, side):
    if step < 0:
        return [(side - 1, 0)]
    if step == 0:
        return [(v, v + 1) for v in range(side)]
    return [(0, side + 1)]


def fine_spread():
    table = np.zeros((9, 2, EDGE, EDGE, 2, TILE), np.float32)
    for j in (-1, 0, 1):
        for l in (-1, 0, 1):
            for y, py in spots(j, EDGE):
                for z, pz in spots(l, EDGE):
                    for x in range(2):
                        table[3 * (j + 1) + l + 1, x, y, z, x, (EDGE + 2) * py + pz] = 1
    return table.reshape(9 * 2 * EDGE * EDGE, 2 * TILE)


def coarse_spread():
    table = np.zeros((10, HALF, HALF, HALF, HALF, TILE), np.float32)
    for j in (-1, 0, 1):
        for l in (-1, 0, 1):
            for y, py in spots(j, HALF):
                for z, pz in spots(l, HALF):
                    for x in range(HALF):
                        table[3 * (j + 1) + l + 1, x, y, z, x, (HALF + 2) * py + pz] = 1
    return table.reshape(10 * HALF**3, HALF * TILE)


def pair_spread():
    centre = coarse_spread().reshape(10, HALF**3, HALF, TILE)[4]
    return np.concatenate([centre, np.roll(centre, 64, axis=-1)]).reshape(2 * HALF**3, HALF * TILE)


def patch_order():
    table = np.zeros((EDGE**3, EDGE**3), np.float32)
    for x in range(EDGE):
        for y in range(EDGE):
            for z in range(EDGE):
                part = 4 * (x % 2) + 2 * (y % 2) + z % 2
                cell = (x // 2 * HALF + y // 2) * HALF + z // 2
                table[(x * EDGE + y) * EDGE + z, part * HALF**3 + cell] = 1
    return table


def dot(a, b):
    return jnp.dot(a, b, preferred_element_type=F32)


def dot_t(a, b):
    return lax.dot_general(a, b, (((1,), (1,)), ((), ())), preferred_element_type=F32)


def split_dot(f, a, b):
    high = a.astype(BF16)
    low = (a - high.astype(F32)).astype(BF16)
    return f(high, b) + f(low, b)


def tiles(x):
    return [x[:, TILE * t : TILE * (t + 1)] for t in range(x.shape[1] // TILE)]


def turn(x, shift):
    shift = shift % TILE
    if shift == 0:
        return x
    return jnp.concatenate([pltpu.roll(t, shift, axis=1) for t in tiles(x)], axis=1)


def sigmoid(v):
    return 1.0 / (1.0 + jnp.exp(-v))


def placed(x, tile_count):
    rows = []
    for a in range(3):
        parts = []
        if a:
            parts.append(jnp.zeros((x.shape[0], a * TILE), x.dtype))
        parts.append(x)
        if a < 2:
            parts.append(jnp.zeros((x.shape[0], (2 - a) * TILE), x.dtype))
        rows.append(jnp.concatenate(parts, axis=1))
    return jnp.concatenate(rows, axis=0)


def group_width(count, peers):
    groups = peers // 2
    return -(-count // (groups * TILE)) * TILE


class Sum:
    def __init__(self, peers, factor, grads, part, pair, mid, got, full, send, recv):
        self.peers, self.factor = peers, factor
        self.grads, self.part, self.pair, self.mid, self.got, self.full = grads, part, pair, mid, got, full
        self.send, self.recv = send, recv
        self.me, self.rep = lax.axis_index("space"), lax.axis_index("rep")
        self.groups = peers // 2
        self.width = part.shape[2]

    def copy(self, src, dst, n, chip, core):
        return pltpu.make_async_remote_copy(
            src_ref=src, dst_ref=dst, send_sem=self.send.at[n], recv_sem=self.recv.at[n],
            device_id=(chip, core), device_id_type=MESH,
        )

    def pair_copy(self):
        other = 1 - self.rep
        src = self.part.at[pl.ds(other * self.peers, self.peers)]
        return self.copy(src, self.pair, 0, self.me, other)

    def share_copy(self, o):
        chip = lax.rem(self.me + o, self.peers)
        return self.copy(self.mid.at[chip], self.got.at[o], o, chip, self.rep)

    def total_copy(self, o, owner):
        chip = lax.rem(self.me + o, self.peers)
        spot = self.full.at[self.rep * self.peers + owner]
        return self.copy(spot, spot, self.peers + o, chip, self.rep)

    def core_copy(self, o):
        owner = lax.rem(self.me + self.peers - o, self.peers)
        spot = self.full.at[self.rep * self.peers + owner]
        return self.copy(spot, spot, 2 * self.peers + o, self.me, 1 - self.rep)

    def each(self, start, act):
        lax.fori_loop(start, self.peers, lambda o, c: (act(o), c)[1], 0)

    def begin(self):
        w = self.width
        for row in range(4):
            for col in range(self.groups):
                self.part[row * self.groups + col] = self.grads[
                    16 * row : 16 * row + 16, col * w : (col + 1) * w
                ].astype(BF16)
        self.pair_copy().start()

    def scatter(self):
        self.pair_copy().wait()
        mine = self.part[pl.ds(self.rep * self.peers, self.peers)]
        self.mid[...] = (mine.astype(F32) + self.pair[...].astype(F32)).astype(BF16)
        self.each(1, lambda o: self.share_copy(o).start())

    def gather(self):
        self.each(1, lambda o: self.share_copy(o).wait())
        total = self.mid[self.me].astype(F32)
        for o in range(1, self.peers):
            total = total + self.got[o].astype(F32)
        self.full[self.rep * self.peers + self.me] = (total * self.factor).astype(BF16)
        self.core_copy(0).start()
        self.each(1, lambda o: self.total_copy(o, self.me).start())

    def forward(self):
        def pass_on(o):
            owner = lax.rem(self.me + self.peers - o, self.peers)
            self.total_copy(o, owner).wait_recv()
            self.core_copy(o).start()

        self.each(1, pass_on)

    def finish(self, out):
        self.each(1, lambda o: self.total_copy(o, self.me).wait_send())
        self.each(0, lambda o: self.core_copy(o).wait())
        out[...] = self.full[...]


def unpack(groups, dec_in, second, first, dec_out, fine, down, coarse, up, sem):
    copy = pltpu.make_async_copy(dec_in, dec_out, sem)
    copy.start()
    for full, outs in ((second, (up, down, coarse)), (first, (fine,))):
        per = full.shape[2] // TILE
        tile = 0
        for out in outs:
            for start in range(0, out.shape[1], TILE):
                size = min(TILE, out.shape[1] - start)
                inner = tile % per * TILE
                for row in range(4):
                    out[16 * row : 16 * row + 16, start : start + size] = full[
                        row * groups + tile // per, :, inner : inner + size
                    ].astype(F32)
                tile += 1
    copy.wait()


def body(
    peers, factor,
    f_ref, nb_ref, sl_ref, cot_ref, w_fine, wd_ref, w_coarse, wu_ref,
    e0_ref, q0_ref, q2_ref, pm_ref,
    out_ref, second_ref, first_ref,
    wf_ref, wc_ref, wct_ref, a0,
    x0, fh, fl, sl_lo, sl_hi, sm_lo, sm_hi, idx, r0, slope0, p2, c2, h1, h1_lo, h1_hi,
    cand, r1, rim, rim_lo, rim_hi, dg0, dgm, dgp, gh1, gh0,
    send_sem, recv_sem, local_sem,
    *sums,
):
    second_sum = Sum(peers, factor, *sums[:8])
    first_sum = Sum(peers, factor, *sums[8:])
    second_grads, first_grads = second_sum.grads, first_sum.grads
    nb, ch = f_ref.shape[0], f_ref.shape[1]
    cells = HALF**3
    me = lax.axis_index("space")
    rep = lax.axis_index("rep")
    up = lax.rem(me + 1, peers)
    down = lax.rem(me + peers - 1, peers)

    barrier = pltpu.get_barrier_semaphore()

    def greet(o, carry):
        other = lax.rem(me + o, peers)
        pl.semaphore_signal(barrier, inc=1, device_id=(other, rep), device_id_type=MESH)
        return carry

    lax.fori_loop(1, peers, greet, 0)
    pl.semaphore_signal(barrier, inc=1, device_id=(me, 1 - rep), device_id_type=MESH)
    pl.semaphore_wait(barrier, peers)

    def remote(src, dst, n, other):
        copy = pltpu.make_async_remote_copy(
            src_ref=src, dst_ref=dst, send_sem=send_sem.at[n], recv_sem=recv_sem.at[n],
            device_id=(other, rep), device_id_type=MESH,
        )
        copy.start()
        return copy

    last = f_ref.shape[2] - TILE
    first = [
        remote(sl_ref, sl_lo, 0, up),
        remote(sl_ref, sl_hi, 1, down),
        remote(f_ref.at[:, :, last:], fh.at[nb : 2 * nb], 2, up),
        remote(f_ref.at[:, :, :TILE], fl.at[nb : 2 * nb], 3, down),
    ]

    x0[:nb] = f_ref[...]
    x0[nb] = jnp.zeros(x0.shape[1:], BF16)
    fh[:nb] = f_ref[:, :, last:]
    fl[:nb] = f_ref[:, :, :TILE]
    fh[2 * nb] = jnp.zeros(fh.shape[1:], BF16)
    fl[2 * nb] = jnp.zeros(fl.shape[1:], BF16)

    def to_patches(src, dst):
        moved = dot(src, pm_ref[...]).astype(BF16)
        for b in range(nb):
            for part in range(8):
                dst[part * ch : (part + 1) * ch, b * cells : (b + 1) * cells] = moved[
                    b * ch : (b + 1) * ch, part * cells : (part + 1) * cells
                ]

    def by_block(value):
        return [value[b * ch : (b + 1) * ch] for b in range(nb)]

    none = 2 * nb
    for b in range(nb):
        for k in range(9, 18):
            v = jnp.int32(b) if k == 13 else nb_ref[b, k if k < 13 else k - 1]
            idx[b, k] = jnp.where(v < 0, nb, v)

    e0 = e0_ref[...]
    e0c = e0_ref[4 * TILE : 5 * TILE, :]
    for b in range(nb):
        for n in range(9):
            for t in range(4):
                row = (4 * b + t) * ch
                a0[row : row + ch, n * TILE : (n + 1) * TILE] = x0[
                    idx[b, 9 + n], :, t * TILE : (t + 1) * TILE
                ]
    inner = dot(a0[...], e0)

    first[0].wait()
    first[1].wait()
    to_smem = [
        pltpu.make_async_copy(sl_lo, sm_lo, local_sem.at[0]),
        pltpu.make_async_copy(sl_hi, sm_hi, local_sem.at[1]),
    ]
    for copy in to_smem:
        copy.start()
    for copy in to_smem:
        copy.wait()
    slots = sl_ref.shape[1]
    for b in range(nb):
        for k in range(9):
            v = nb_ref[b, k]
            far = nb + sm_lo[0, jnp.clip(v - nb, 0, slots - 1)]
            idx[b, k] = jnp.where(v < 0, none, jnp.where(v < nb, v, far))
        for k in range(18, 27):
            v = nb_ref[b, k - 1]
            far = nb + sm_hi[1, jnp.clip(v - nb - slots, 0, slots - 1)]
            idx[b, k] = jnp.where(v < 0, none, jnp.where(v < nb, v, far))
    taps = 9 * ch
    for a in range(3):
        wf_ref[a * ch : (a + 1) * ch, :] = w_fine[:, a * taps : (a + 1) * taps]
        wc_ref[a * ch : (a + 1) * ch, :] = w_coarse[:, a * taps : (a + 1) * taps]
    for n in range(0, 27, 2):
        size = min(2, 27 - n)
        turned = w_coarse[:, n * ch : (n + size) * ch].astype(F32).T.astype(BF16)
        for m in range(size):
            a, k = (n + m) // 9, (n + m) % 9
            wct_ref[a * ch : (a + 1) * ch, k * ch : (k + 1) * ch] = turned[m * ch : (m + 1) * ch]
    wdt = wd_ref[...].astype(F32).T.astype(BF16)
    wut = wu_ref[...].astype(F32).T.astype(BF16)
    to_patches(jnp.concatenate([cot_ref[b] for b in range(nb)], axis=0), c2)

    first[2].wait()
    first[3].wait()

    def faces(table, i):
        return jnp.concatenate(
            [
                jnp.concatenate([table[idx[b, 9 * i + n]] for n in range(9)], axis=1)
                for b in range(nb)
            ],
            axis=0,
        )

    low = by_block(dot(faces(fh, 0), e0[:, TILE:]))
    high = by_block(dot(faces(fl, 2), e0[:, :TILE]))
    wide = EDGE * TILE
    span = wide + 2 * TILE
    hidden0 = []
    for b in range(nb):
        middle = [inner[(4 * b + t) * ch : (4 * b + t + 1) * ch] for t in range(4)]
        pad = jnp.concatenate([low[b]] + middle + [high[b]], axis=1)
        for n in range(9):
            off = (EDGE + 2) * (n // 3 - 1) + n % 3 - 1
            r0[n * ch : (n + 1) * ch, b * span : (b + 1) * span] = turn(pad, -off).astype(BF16)
        y = dot(wf_ref[...], r0[:, b * span : (b + 1) * span])
        v = sum(y[a * ch : (a + 1) * ch, a * TILE : a * TILE + wide] for a in range(3))
        s = sigmoid(v)
        slope0[b] = s * (1.0 + v * (1.0 - s))
        h = (v * s).astype(BF16)
        hidden0 += [h[:, 2 * TILE * t : 2 * TILE * (t + 1)] for t in range(4)]
    flat = dot_t(jnp.concatenate(hidden0, axis=0), e0c).astype(BF16)

    def rows_to_lanes(value):
        return jnp.concatenate(
            [
                jnp.concatenate(
                    [value[(4 * b + t) * ch : (4 * b + t + 1) * ch] for t in range(4)], axis=1
                )
                for b in range(nb)
            ],
            axis=0,
        )

    to_patches(rows_to_lanes(flat), p2)

    coarse_pre = dot(wd_ref[...], p2[...])
    s = sigmoid(coarse_pre)
    slope_down = s * (1.0 + coarse_pre * (1.0 - s))
    hidden1 = (coarse_pre * s).astype(BF16)
    h1[...] = hidden1
    second = [remote(h1, h1_lo, 4, up), remote(h1, h1_hi, 5, down)]

    lane = lax.broadcasted_iota(jnp.int32, (ch, TILE), 1)
    left = lane < cells
    nothing = jnp.zeros((ch, TILE), F32)

    def candidates(value, table, base):
        for b in range(nb):
            x = value[:, (b // 2) * TILE : (b // 2 + 1) * TILE].astype(F32)
            swapped = pltpu.roll(x, cells, axis=1)
            on_left, on_right = (x, swapped) if b % 2 == 0 else (swapped, x)
            cand[table, 0, base + b] = jnp.where(left, on_left, nothing).astype(BF16)
            cand[table, 1, base + b] = jnp.where(left, nothing, on_right).astype(BF16)

    for table in range(3):
        candidates(hidden1, table, 0)
        for half in range(2):
            cand[table, half, none] = nothing.astype(BF16)
            if table == 1:
                for n in range(nb, 2 * nb):
                    cand[table, half, n] = nothing.astype(BF16)
    up_back = dot(wu_ref[...], c2[...])
    q0 = q0_ref[...]
    top = (HALF - 1) * TILE

    def sources(i):
        rows = []
        for b in range(nb):
            parts = []
            for t in range(5):
                x = cand[i, 0, idx[b, 9 * i + 2 * t]]
                if t < 4:
                    x = x + cand[i, 1, idx[b, 9 * i + 2 * t + 1]]
                parts.append(x)
            rows.append(jnp.concatenate(parts, axis=1))
        return jnp.concatenate(rows, axis=0)

    pairs = nb // 2
    wide1 = HALF * TILE
    inner1 = dot(sources(1), q0)
    for copy in second:
        copy.wait()
    candidates(h1_lo[...], 0, nb)
    candidates(h1_hi[...], 2, nb)

    pads = by_block(
        jnp.concatenate(
            [dot(sources(0), q0[:, top:]), inner1, dot(sources(2), q0[:, :TILE])],
            axis=1,
        )
    )
    pre, ups = [], []
    for p in range(pairs):
        pad = pads[2 * p] + turn(pads[2 * p + 1], cells)
        for n in range(9):
            off = (HALF + 2) * (n // 3 - 1) + n % 3 - 1
            r1[p, n * ch : (n + 1) * ch, :] = turn(pad, -off).astype(BF16)
        y = dot(wc_ref[...], r1[p])
        pre.append(sum(y[a * ch : (a + 1) * ch, a * TILE : a * TILE + wide1] for a in range(3)))
        ups.append(up_back[:, p * TILE : (p + 1) * TILE])
    v = jnp.concatenate(pre, axis=0)
    s = sigmoid(v)
    slope = s * (1.0 + v * (1.0 - s))
    gated = dot_t((v * s).astype(BF16), q2_ref[...]).astype(BF16)
    delta = (split_dot(dot, jnp.concatenate(ups, axis=0), q2_ref[...]) * slope).astype(BF16)
    delta_up = [delta[p * ch : (p + 1) * ch] for p in range(pairs)]
    gated = jnp.concatenate([gated[p * ch : (p + 1) * ch] for p in range(pairs)], axis=1)
    gap = jnp.zeros((ch, TILE), F32)
    backs = []
    for p in range(pairs):
        turned = []
        for n in range(9):
            off = (HALF + 2) * (n // 3 - 1) + n % 3 - 1
            turned.append(turn(delta_up[p].astype(F32), off).astype(BF16))
        y = dot(wct_ref[...], jnp.concatenate(turned, axis=0))
        back = (
            jnp.concatenate([y[:ch], gap, gap], axis=1)
            + jnp.concatenate([gap, y[ch : 2 * ch], gap], axis=1)
            + jnp.concatenate([gap, gap, y[2 * ch :]], axis=1)
        )
        rim[0, p] = back[:, :TILE].astype(BF16)
        rim[1, p] = back[:, -TILE:].astype(BF16)
        backs += [back, turn(back, -cells)]
    third = [remote(rim.at[0], rim_hi, 6, down), remote(rim.at[1], rim_lo, 7, up)]

    backs = jnp.concatenate(backs, axis=0)
    for table, value, spread in (
        (dg0, backs[:, TILE : TILE + wide1], q0),
        (dgm, backs[:, :TILE], q0[:, top:]),
        (dgp, backs[:, -TILE:], q0[:, :TILE]),
    ):
        for b, x in enumerate(by_block(dot_t(value.astype(BF16), spread))):
            table[b] = x

    dec = (p2[...].astype(F32) + dot(wut, gated)).astype(BF16)

    def from_patches(value):
        return jnp.concatenate(
            [
                jnp.concatenate(
                    [
                        value[n * ch : (n + 1) * ch, b * cells : (b + 1) * cells]
                        for n in range(8)
                    ],
                    axis=1,
                )
                for b in range(nb)
            ],
            axis=0,
        )

    for b, x in enumerate(by_block(dot_t(from_patches(dec), pm_ref[...]).astype(BF16))):
        out_ref[b] = x
    held = 8 * ch
    second_grads[:, :held] = dot_t(gated, c2[...])
    grad_coarse = sum(dot_t(placed(delta_up[p], HALF), r1[p]) for p in range(pairs))
    for a in range(3):
        start = 2 * held + a * taps
        second_grads[:, start : start + taps] = grad_coarse[a * ch : (a + 1) * ch]
    for ref, used in ((first_grads, 3 * taps), (second_grads, 3 * taps + 2 * held)):
        ref[:, used:] = jnp.zeros((ch, ref.shape[1] - used), F32)

    dg0[nb] = jnp.zeros(dg0.shape[1:], F32)
    dgm[none] = jnp.zeros(dg0.shape[1:], F32)
    dgp[none] = jnp.zeros(dg0.shape[1:], F32)
    for copy in third:
        copy.wait()
    for table, ref, spread in ((dgm, rim_hi, q0[:, top:]), (dgp, rim_lo, q0[:, :TILE])):
        rows = []
        for p in range(pairs):
            x = ref[p].astype(F32)
            rows += [x, turn(x, -cells)]
        rows = jnp.concatenate(rows, axis=0).astype(BF16)
        for b, x in enumerate(by_block(dot_t(rows, spread))):
            table[nb + b] = x
    for b in range(nb):
        sums = [nothing, nothing]
        for k in range(27):
            chunk = 8 - k % 9
            table = (dgp, dg0, dgm)[k // 9]
            t = chunk // 2
            sums[chunk % 2] = sums[chunk % 2] + table[idx[b, k], :, t * TILE : (t + 1) * TILE]
        gh1[:, b * cells : (b + 1) * cells] = sums[0][:, :cells] + sums[1][:, cells:]
    delta_down = (gh1[...] * slope_down).astype(BF16)
    second_grads[:, held : 2 * held] = dot_t(delta_down, p2[...])
    second_sum.begin()
    gh0[...] = c2[...].astype(F32) + dot(wdt, delta_down)
    flat = dot_t(from_patches(gh0[...]).astype(BF16), pm_ref[...]).astype(BF16)
    spread = jnp.concatenate(
        [flat[b * ch : (b + 1) * ch, t * TILE : (t + 1) * TILE] for b in range(nb) for t in range(4)],
        axis=0,
    )
    wide_grad = by_block(rows_to_lanes(dot(spread, e0c)))
    second_sum.scatter()
    grad_fine = jnp.zeros((3 * ch, taps), F32)
    for b in range(nb):
        delta = (wide_grad[b] * slope0[b]).astype(BF16)
        grad_fine = grad_fine + dot_t(placed(delta, EDGE), r0[:, b * span : (b + 1) * span])
        if b == nb // 2:
            second_sum.gather()
    for a in range(3):
        first_grads[:, a * taps : (a + 1) * taps] = grad_fine[a * ch : (a + 1) * ch]
    first_sum.begin()
    first_sum.scatter()
    second_sum.forward()
    first_sum.gather()
    second_sum.finish(second_ref)
    first_sum.forward()
    first_sum.finish(first_ref)


def shards(features, neighbours, send_list, w_fine, w_down, w_coarse, w_up, cotangent):
    nb, ch = features.shape[1], features.shape[2]
    cols = nb * HALF**3
    peers = lax.axis_size("space")
    taps = 9 * ch

    consts = [jnp.asarray(t(), BF16) for t in (fine_spread, coarse_spread, pair_spread, patch_order)]
    vmem = pl.BlockSpec(memory_space=pltpu.VMEM)
    smem = pl.BlockSpec(memory_space=pltpu.SMEM)
    v = pltpu.VMEM
    width = 10 * HALF**3
    factor = 1.0 / math.sqrt(lax.axis_size("rep") * peers * nb * EDGE**3)

    def sum_buffers(share):
        return [
            v((ch, peers // 2 * share), F32),
            v((2 * peers, 16, share), BF16),
            v((peers, 16, share), BF16),
            v((peers, 16, share), BF16),
            v((peers, 16, share), BF16),
            v((2 * peers, 16, share), BF16),
            pltpu.SemaphoreType.DMA((3 * peers,)),
            pltpu.SemaphoreType.DMA((3 * peers,)),
        ]

    shares = [group_width(n, peers) for n in (3 * taps + 16 * ch, 3 * taps)]
    half_done = pl.pallas_call(
        functools.partial(body, peers, factor),
        out_shape=(
            jax.ShapeDtypeStruct(features.shape[1:], BF16),
            *[jax.ShapeDtypeStruct((2 * peers, 16, share), BF16) for share in shares],
        ),
        in_specs=[vmem, smem] + [vmem] * 10,
        out_specs=(vmem,) * 3,
        scratch_shapes=[
            v((3 * ch, taps), BF16),
            v((3 * ch, taps), BF16),
            v((3 * ch, taps), BF16),
            v((4 * nb * ch, 9 * TILE), BF16),
            v((nb + 1, ch, EDGE**3), BF16),
            v((2 * nb + 1, ch, TILE), BF16),
            v((2 * nb + 1, ch, TILE), BF16),
            v(send_list.shape[2:], jnp.int32),
            v(send_list.shape[2:], jnp.int32),
            pltpu.SMEM(send_list.shape[2:], jnp.int32),
            pltpu.SMEM(send_list.shape[2:], jnp.int32),
            pltpu.SMEM((nb, 27), jnp.int32),
            v((taps, nb * (EDGE + 2) * TILE), BF16),
            v((nb, ch, EDGE * TILE), F32),
            v((8 * ch, cols), BF16),
            v((8 * ch, cols), BF16),
            v((ch, cols), BF16),
            v((ch, cols), BF16),
            v((ch, cols), BF16),
            v((3, 2, 2 * nb + 1, ch, TILE), BF16),
            v((nb // 2, taps, (HALF + 2) * TILE), BF16),
            v((2, nb // 2, ch, TILE), BF16),
            v((nb // 2, ch, TILE), BF16),
            v((nb // 2, ch, TILE), BF16),
            v((nb + 1, ch, width), F32),
            v((2 * nb + 1, ch, width), F32),
            v((2 * nb + 1, ch, width), F32),
            v((ch, cols), F32),
            v((8 * ch, cols), F32),
            pltpu.SemaphoreType.DMA((8,)),
            pltpu.SemaphoreType.DMA((8,)),
            pltpu.SemaphoreType.DMA((2,)),
            *sum_buffers(shares[0]),
            *sum_buffers(shares[1]),
        ],
        compiler_params=pltpu.CompilerParams(
            collective_id=0, has_side_effects=True, vmem_limit_bytes=56 * 1024 * 1024
        ),
    )(
        features[0], neighbours[0], send_list[0, 0], cotangent[0],
        w_fine, w_down, w_coarse, w_up, *consts,
    )
    anywhere = pl.BlockSpec(memory_space=pl.ANY)
    decoded, *grads = pl.pallas_call(
        functools.partial(unpack, peers // 2),
        out_shape=(
            jax.ShapeDtypeStruct(features.shape[1:], BF16),
            *[jax.ShapeDtypeStruct(w.shape, F32) for w in (w_fine, w_down, w_coarse, w_up)],
        ),
        in_specs=[anywhere, vmem, vmem],
        out_specs=(anywhere, vmem, vmem, vmem, vmem),
        scratch_shapes=[pltpu.SemaphoreType.DMA],
        compiler_params=pltpu.CompilerParams(vmem_limit_bytes=60 * 1024 * 1024),
    )(*half_done)
    return decoded[None], *grads


def solution(mesh):
    in_specs = (
        P("rep", "space", None, None),
        P("rep", "space", None),
        P("rep", "space", None, None),
        P(),
        P(),
        P(),
        P(),
        P("rep", "space", None, None),
    )
    out_specs = (P("rep", "space", None, None), P(), P(), P(), P())
    return jax.shard_map(shards, mesh=mesh, in_specs=in_specs, out_specs=out_specs, check_vma=False)
```
